128 devices in a mesh: seq: 32 (over z_hi, x, y), head: 4 (over z_lo, core).
Axes of the slice: x: 4, y: 4, z: 4 (z_hi: 2, z_lo: 2; z = z_hi * 2 + z_lo), core: 2. Of those that a mesh axis runs over, the one named last changes fastest.
Arguments:
- visual: bfloat16 [8192, 3584], P('seq', 'head'), may hold values from -60 to 60
- frame_source: int32 [512], replicated, may hold values from 0 to 511, as said below
- input_norm_gain: bfloat16 [3584], replicated, may hold values from 0.099609375 to 1.8984375
- w_query: bfloat16 [3584, 3584], P(None, 'head'), may hold values from -0.09375 to 0.09375
- w_key: bfloat16 [3584, 512], P(None, 'head'), may hold values from -0.09375 to 0.09375
- w_value: bfloat16 [3584, 512], P(None, 'head'), may hold values from -0.09375 to 0.09375
- q_bias: bfloat16 [3584], P('head'), may hold values from -12 to 12
- k_bias: bfloat16 [512], P('head'), may hold values from -12 to 12
- v_bias: bfloat16 [512], P('head'), may hold values from -4 to 4
- w_out: bfloat16 [3584, 3584], P('head'), may hold values from -0.09375 to 0.09375
Outputs:
- attended: bfloat16 [8192, 3584], P(('seq', 'head'))
The draws below stay inside these ranges and needn't reach their ends.
Inputs may be any that keep to these rules, and one draw needn't show every extreme that they name: `frame_source`: A permutation of the 512 encoder frames. Of the 16 frames that one index of seq holds in the layout order, at most 1 come from the 16 encoder frames of one index, and exactly 1 for some pair of indices in every draw.
All inputs are finite; a program needn't handle non-finite values.
Results may differ from the reference program's by a relative error of at most 0.0095.
The reference program's roundings to bfloat16 on the way count: a program that leaves them out, or rounds other values in their place, can miss the bound.
Values may be sent and summed in bfloat16 or wider, within the bound.
A program may use at most 128 MiB of HBM per device.

```python
import math
import jax
import jax.numpy as jnp
from jax import lax

D = 3584
QH = 28
KVH = 4
HD = 128
FT = 16
FR_DEV = 16
FRAMES = 512
N_SEQ = 32


def draw_q_bias(key, part):
    key = jax.random.fold_in(key, 21)
    noise = jax.random.truncated_normal(key, -4.0, 4.0, (QH, HD), jnp.float32)
    return (0.7 * noise).reshape(QH * HD).astype(jnp.bfloat16)


def draw_k_bias(key, part):
    key = jax.random.fold_in(key, 22)
    noise = jax.random.truncated_normal(key, -4.0, 4.0, (KVH, HD), jnp.float32)
    return (0.7 * noise).reshape(KVH * HD).astype(jnp.bfloat16)


def draw_visual(key, part):
    key = jax.random.fold_in(key, 23)
    first, second = jax.random.split(key, 2)
    count = FRAMES * FT
    base = jax.random.truncated_normal(first, -4.0, 4.0, (count, D), jnp.float32)
    row_scale = jnp.exp(jax.random.uniform(second, (count, 1), jnp.float32, math.log(0.3), math.log(3.0)))
    return (base * row_scale).astype(jnp.bfloat16)


def draw_frame_source(key, part):
    key = jax.random.fold_in(key, 11)
    keys = jax.random.split(key, 5)
    count = N_SEQ
    per_dev = FR_DEV
    offsets = jax.random.permutation(keys[0], count)[jnp.arange(per_dev) % count]
    alpha = jax.random.permutation(keys[1], count)
    beta = jax.random.permutation(keys[2], count)
    orders = jax.vmap(lambda each: jax.random.permutation(each, per_dev))(jax.random.split(keys[3], count))
    slots = jax.vmap(lambda each: jax.random.permutation(each, per_dev))(jax.random.split(keys[4], count))
    owners = jnp.arange(count, dtype=jnp.int32)[:, None]
    places = jnp.arange(per_dev, dtype=jnp.int32)[None, :]
    request = orders.astype(jnp.int32)
    source = alpha[(beta[owners] + offsets[request]) % count].astype(jnp.int32)
    slot = slots[source, request].astype(jnp.int32)
    half_frames = per_dev // 2
    sequence_frame = jnp.where(places < half_frames, owners * half_frames + places, (2 * count - 1 - owners) * half_frames + places - half_frames)
    result = jnp.zeros((count * per_dev,), jnp.int32)
    return result.at[sequence_frame.reshape(-1)].set((source * per_dev + slot).reshape(-1))


def steps_of(stream_key, shape, pieces, smallest, top_value):
    def one(axis_at, blocks):
        steps = jax.random.uniform(jax.random.fold_in(jax.random.fold_in(stream_key, 6), axis_at), (blocks,), jnp.float32, smallest / len(pieces), top_value / len(pieces))
        return jnp.repeat(jnp.exp(steps), shape[axis_at] // blocks).reshape((-1,) + (1,) * (len(shape) - axis_at - 1))

    loudness = one(*pieces[0])
    for cut in pieces[1:]:
        loudness = loudness * one(*cut)
    return loudness


def gaussian(stream_key, extent, deviation, reach, pieces=(), kind=jnp.bfloat16):
    level = steps_of(stream_key, extent, pieces, -0.22, 0.18) if pieces else 1.0
    values = jax.random.normal(stream_key, extent, jnp.float32) * deviation * level
    return jnp.minimum(jnp.maximum(values, -reach), reach).astype(kind)


def setup_inputs(seed: int = 0) -> dict:
    key_list = jax.random.split(jax.random.key(seed), 11)
    return {
        "visual": draw_visual(jax.random.fold_in(key_list[10], 71), 0),
        "frame_source": draw_frame_source(jax.random.fold_in(key_list[10], 71), 0),
        "input_norm_gain": jnp.clip(1.0 + 0.18 * jax.random.normal(key_list[2], (D,), jnp.float32), 0.099609375, 1.8984375).astype(jnp.bfloat16),
        "w_query": gaussian(key_list[3], (D, QH * HD), D ** -0.5, 0.09375, ((1, 4),)),
        "w_key": gaussian(key_list[4], (D, KVH * HD), D ** -0.5, 0.09375, ((1, 4),)),
        "w_value": gaussian(key_list[5], (D, KVH * HD), D ** -0.5, 0.09375, ((1, 4),)),
        "q_bias": draw_q_bias(jax.random.fold_in(key_list[10], 71), 0),
        "k_bias": draw_k_bias(jax.random.fold_in(key_list[10], 71), 0),
        "v_bias": gaussian(key_list[8], (KVH * HD,), 0.7, 4.0, ((0, 4),)),
        "w_out": gaussian(key_list[9], (QH * HD, D), (QH * HD) ** -0.5, 0.09375, ((0, 4),)),
    }


def rotate(values_in, positions, head_size):
    half_size = head_size // 2
    inverse = 1000000.0 ** (-(jnp.arange(half_size, dtype=jnp.float32) * 2.0) / head_size)
    angle = positions.astype(jnp.float32)[:, None] * inverse[None, :]
    cosine = jnp.concatenate([jnp.cos(angle), jnp.cos(angle)], axis=-1)[:, None, :]
    sine = jnp.concatenate([jnp.sin(angle), jnp.sin(angle)], axis=-1)[:, None, :]
    first = values_in[..., :half_size]
    second = values_in[..., half_size:]
    turned = jnp.concatenate([-second, first], axis=-1)
    return values_in * cosine + turned * sine

def reference(visual, frame_source, input_norm_gain, w_query, w_key, w_value, q_bias, k_bias, v_bias, w_out):
    length = FRAMES * FT
    rows = visual.reshape(FRAMES, FT, D)[frame_source].reshape(length, D)
    floats = rows.astype(jnp.float32)
    spread = lax.optimization_barrier(jnp.mean(floats * floats, axis=-1, keepdims=True))
    normed = (floats * lax.rsqrt(spread + 1e-06) * input_norm_gain.astype(jnp.float32)).astype(jnp.bfloat16)
    positions = jnp.arange(length, dtype=jnp.int32)
    queries = jnp.dot(normed, w_query, preferred_element_type=jnp.float32) + q_bias.astype(jnp.float32)
    keys = jnp.dot(normed, w_key, preferred_element_type=jnp.float32) + k_bias.astype(jnp.float32)
    values = jnp.dot(normed, w_value, preferred_element_type=jnp.float32) + v_bias.astype(jnp.float32)
    queries = rotate(queries.reshape(length, QH, HD), positions, HD).astype(jnp.bfloat16)
    keys = rotate(keys.reshape(length, KVH, HD), positions, HD).astype(jnp.bfloat16)
    values = values.astype(jnp.bfloat16).reshape(length, KVH, HD)
    group = QH // KVH
    grouped_heads = queries.reshape(length, KVH, group, HD)
    block_size = math.gcd(length, 1024)
    scale = 1.0 / math.sqrt(HD)

    def per_head(head_index):
        head_queries = lax.dynamic_index_in_dim(grouped_heads, head_index, 1, keepdims=False)
        head_keys = lax.dynamic_index_in_dim(keys, head_index, 1, keepdims=False).astype(jnp.float32)
        head_values = lax.dynamic_index_in_dim(values, head_index, 1, keepdims=False).astype(jnp.float32)

        def rows_per_block(block_index):
            first_row = (block_index * block_size).astype(jnp.int32)
            block_queries = lax.dynamic_slice_in_dim(head_queries, first_row, block_size, 0).astype(jnp.float32)
            scores = jnp.einsum('qgd,kd->gqk', block_queries, head_keys) * scale
            query_pos = first_row + jnp.arange(block_size, dtype=jnp.int32)
            causal_visible = positions[None, :] <= query_pos[:, None]
            scores = jnp.where(causal_visible[None], scores, -1e+30)
            top = lax.optimization_barrier(jnp.max(scores, axis=-1, keepdims=True))
            expo = jnp.where(causal_visible[None], jnp.exp(scores - top), 0.0)
            total = lax.optimization_barrier(jnp.sum(expo, axis=-1))
            rounded = lax.optimization_barrier(expo.astype(jnp.bfloat16)).astype(jnp.float32)
            summed = jnp.einsum('gqk,kd->gqd', rounded, head_values)
            return (summed / total[..., None]).astype(jnp.bfloat16)
        blocks = lax.map(rows_per_block, jnp.arange(length // block_size, dtype=jnp.int32))
        return jnp.transpose(blocks, (0, 2, 1, 3)).reshape(length, group, HD)
    heads = lax.map(per_head, jnp.arange(KVH, dtype=jnp.int32))
    heads_out = jnp.transpose(heads, (1, 0, 2, 3)).reshape(length, QH * HD)
    result = jnp.dot(heads_out, w_out, preferred_element_type=jnp.float32).astype(jnp.bfloat16)
    half_frames = FR_DEV // 2
    device_ids = jnp.arange(N_SEQ, dtype=jnp.int32)[:, None]
    local_ids = jnp.arange(FR_DEV, dtype=jnp.int32)[None, :]
    layout = jnp.where(local_ids < half_frames, device_ids * half_frames + local_ids, (2 * N_SEQ - 1 - device_ids) * half_frames + local_ids - half_frames).reshape(-1)
    return result.reshape(FRAMES, FT, D)[layout].reshape(length, D)
```

```python
import functools
import math

import jax
import jax.numpy as jnp
from jax import lax
from jax.experimental import pallas as pl
from jax.experimental.pallas import tpu as pltpu
from jax.sharding import PartitionSpec as P

HD = 128
FT = 16
FR_DEV = 16
TOK_DEV = 256
BLOCK = 128
MESH = pl.DeviceIdType.MESH
NEG = -1e30
EXP_SCALE = math.log2(math.e) / math.sqrt(HD)


def rotate(values_in, positions, head_size):
    half_size = head_size // 2
    inverse = 1000000.0 ** (-(jnp.arange(half_size, dtype=jnp.float32) * 2.0) / head_size)
    angle = positions.astype(jnp.float32)[:, None] * inverse[None, :]
    cosine = jnp.concatenate([jnp.cos(angle), jnp.cos(angle)], axis=-1)[:, None, :]
    sine = jnp.concatenate([jnp.sin(angle), jnp.sin(angle)], axis=-1)[:, None, :]
    first = values_in[..., :half_size]
    second = values_in[..., half_size:]
    turned = jnp.concatenate([-second, first], axis=-1)
    return values_in * cosine + turned * sine


def layout_frame(device_ids, local_ids, seq_count):
    half_frames = FR_DEV // 2
    return jnp.where(
        local_ids < half_frames,
        device_ids * half_frames + local_ids,
        (2 * seq_count - 1 - device_ids) * half_frames + local_ids - half_frames,
    )


def layout_positions(first_row, count, seq_count):
    row_ids = first_row + jnp.arange(count, dtype=jnp.int32)
    device_ids = row_ids // TOK_DEV
    device_local_rows = row_ids % TOK_DEV
    frame_ids = layout_frame(device_ids, device_local_rows // FT, seq_count)
    return frame_ids * FT + device_local_rows % FT


def on_device(
    visual, frame_source, input_norm_gain, w_query, w_key, w_value, q_bias, k_bias, v_bias, w_out
):
    seq_count = lax.axis_size("seq")
    seq_index = lax.axis_index("seq")
    capacity = (FR_DEV + seq_count - 1) // seq_count
    half_frames = FR_DEV // 2
    frame_ids = jnp.arange(frame_source.shape[0], dtype=jnp.int32)
    block_ids = frame_ids // half_frames
    owner = jnp.where(block_ids < seq_count, block_ids, 2 * seq_count - 1 - block_ids)
    local_place = frame_ids % half_frames + jnp.where(block_ids < seq_count, 0, half_frames)
    source_dev = frame_source // FR_DEV
    source_slot = frame_source % FR_DEV
    earlier = (
        (owner[:, None] == owner[None, :])
        & (source_dev[:, None] == source_dev[None, :])
        & (local_place[None, :] < local_place[:, None])
    )
    rank = jnp.sum(earlier.astype(jnp.int32), axis=1)
    target = jnp.where(source_dev == seq_index, owner * capacity + rank, seq_count * capacity)
    send_slot = (
        jnp.zeros((seq_count * capacity,), jnp.int32).at[target].set(source_slot, mode="drop")
    )
    send_live = jnp.zeros((seq_count * capacity,), jnp.bool_).at[target].set(True, mode="drop")
    own_frames = layout_frame(seq_index, jnp.arange(FR_DEV, dtype=jnp.int32), seq_count)
    receive_index = source_dev[own_frames] * capacity + rank[own_frames]
    picked = visual.reshape(FR_DEV, FT, visual.shape[1])[send_slot]
    moved = lax.all_to_all(
        jnp.where(send_live[:, None, None], picked, jnp.zeros_like(picked)),
        "seq",
        split_axis=0,
        concat_axis=0,
        tiled=True,
    )
    placed = moved[receive_index].reshape(TOK_DEV, visual.shape[1])
    hidden = lax.all_gather(placed, "head", axis=1, tiled=True)
    floats = hidden.astype(jnp.float32)
    spread = jnp.mean(floats * floats, axis=-1, keepdims=True)
    normed = (floats * lax.rsqrt(spread + 1e-06) * input_norm_gain.astype(jnp.float32)).astype(
        jnp.bfloat16
    )
    query_heads = w_query.shape[1] // HD
    value_heads = w_key.shape[1] // HD
    positions = layout_positions(seq_index * TOK_DEV, TOK_DEV, seq_count)
    queries = jnp.dot(normed, w_query, preferred_element_type=jnp.float32) + q_bias.astype(
        jnp.float32
    )
    keys_local = jnp.dot(normed, w_key, preferred_element_type=jnp.float32) + k_bias.astype(
        jnp.float32
    )
    values_local = jnp.dot(normed, w_value, preferred_element_type=jnp.float32) + v_bias.astype(
        jnp.float32
    )
    queries = rotate(queries.reshape(TOK_DEV, query_heads, HD), positions, HD).astype(jnp.bfloat16)
    keys_local = rotate(keys_local.reshape(TOK_DEV, value_heads, HD), positions, HD).astype(
        jnp.bfloat16
    )
    keys_local = keys_local.reshape(TOK_DEV, value_heads * HD)
    values_local = values_local.astype(jnp.bfloat16)
    q = jnp.transpose(queries.reshape(2, BLOCK, query_heads, HD), (0, 2, 1, 3))
    kv = jnp.stack(
        [keys_local.reshape(2, BLOCK, HD), values_local.reshape(2, BLOCK, HD)], axis=1
    )
    heads_out = attend(q.reshape(2, query_heads * BLOCK, HD), kv)
    heads_out = heads_out.reshape(TOK_DEV, query_heads * HD)
    picked = heads_out
    summed = lax.psum_scatter(
        jnp.dot(picked, w_out, preferred_element_type=jnp.float32),
        "head",
        scatter_dimension=0,
        tiled=True,
    )
    return summed.astype(jnp.bfloat16)


def coordinates():
    me = lax.axis_index("seq")
    return me, me // 16, (me // 4) % 4, me % 4


def near(dz, dx, dy):
    _, z, x, y = coordinates()
    return ((z + dz) % 2) * 16 + ((x + dx) % 4) * 4 + (y + dy) % 4


def gather_plan():
    plan = []
    for block in range(2):
        for dz in range(2):
            for dx in range(4):
                for dy in range(4):
                    if dz == dx == dy == 0:
                        continue
                    first, last = (dx, dy) if block == 0 else (dy, dx)
                    depth = dz + min(first, 4 - first) + min(last, 4 - last)
                    sends = []
                    if last == 0:
                        if first == 0:
                            sends += [(0, 1), (0, 3)]
                        if (first == 3 and dz == 0) or (first == 1 and dz == 1):
                            sends += [(0, 4 - first)]
                        sends += [(1, 1), (1, 3)]
                    elif (last == 3 and dz == 0) or (last == 1 and dz == 1):
                        sends += [(1, 4 - last)]
                    targets = []
                    for which, step in sends:
                        along_x = (which == 0) == (block == 0)
                        targets.append((0, step, 0) if along_x else (0, 0, step))
                    plan.append((depth, block, (dz, dx, dy), targets))
    plan.sort(key=lambda entry: (entry[0], entry[2][0], entry[2][1] == 2, entry[2][2] == 2))
    return plan


def attend_unit(q, buf, m, l, acc, which, group, block, keep):
    keys = buf[pl.ds(group * 4, 4), block, 0].reshape(4 * BLOCK, HD)
    vals = buf[pl.ds(group * 4, 4), block, 1].reshape(4 * BLOCK, HD)
    s = lax.dot_general(
        q[which], keys, (((1,), (1,)), ((), ())), preferred_element_type=jnp.float32
    )
    if keep is not None:
        s = jnp.where(keep, s, NEG)
    old = m[which]
    new = jnp.maximum(old, jnp.max(s, axis=1, keepdims=True))
    fade = jnp.exp2((old - new) * EXP_SCALE)
    p = jnp.exp2((s - jnp.concatenate([new] * 4, axis=1)) * EXP_SCALE)
    parts = p[:, :128] + p[:, 128:256] + p[:, 256:384] + p[:, 384:]
    l[which] = l[which] * fade + parts
    acc[which] = acc[which] * fade + jnp.dot(
        p.astype(jnp.bfloat16), vals, preferred_element_type=jnp.float32
    )
    m[which] = new


def attend_kernel(q, kv, o, buf, m, l, acc, send_sem, recv_sem):
    me, z, x, y = coordinates()
    head = lax.axis_index("head")
    own = me // 4
    partners = [(1, 0, 0), (0, 1, 0), (0, 3, 0), (0, 0, 1), (0, 0, 3)]
    barrier = pltpu.get_barrier_semaphore()
    for partner in partners:
        pl.semaphore_signal(
            barrier, inc=1, device_id=(near(*partner), head), device_id_type=MESH
        )
    buf[me] = kv[...]
    m[...] = jnp.full_like(m, NEG)
    l[...] = jnp.zeros_like(l)
    acc[...] = jnp.zeros_like(acc)
    pl.semaphore_wait(barrier, len(partners))

    started = []

    def send(source, block, target):
        index = near(*source)
        copy = pltpu.make_async_remote_copy(
            src_ref=buf.at[index, block],
            dst_ref=buf.at[index, block],
            send_sem=send_sem.at[len(started)],
            recv_sem=recv_sem.at[index, block],
            device_id=(near(*target), head),
            device_id_type=MESH,
        )
        copy.start()
        started.append(copy)

    def arrive(source, block):
        index = near(*source)
        pltpu.make_async_remote_copy(
            src_ref=buf.at[index, block],
            dst_ref=buf.at[index, block],
            send_sem=send_sem.at[0],
            recv_sem=recv_sem.at[index, block],
            device_id=(near(1, 0, 0), head),
            device_id_type=MESH,
        ).wait_recv()

    for block in range(2):
        send((0, 0, 0), block, (1, 0, 0))
    for block in range(2):
        for partner in partners[1:]:
            send((0, 0, 0), block, partner)

    waiting = {}
    for dz in range(2):
        for dx in range(4):
            waiting[dz, dx] = 8 if (dz, dx) != (0, 0) else 6

    def attend(dz, dx):
        group = near(dz, dx, 0) // 4
        unit = functools.partial(attend_unit, q, buf, m, l, acc)
        if (dz, dx) == (0, 0):
            row = lax.broadcasted_iota(jnp.int32, (7, BLOCK, 4 * BLOCK), 1)
            row = row.reshape(7 * BLOCK, 4 * BLOCK) + y * BLOCK
            column = lax.broadcasted_iota(jnp.int32, (7 * BLOCK, 4 * BLOCK), 1)
            unit(0, group, 0, column <= row)
            unit(1, group, 0, None)
            later = column % BLOCK - (column // BLOCK) * BLOCK
            unit(1, group, 1, later <= row - 2 * y * BLOCK)
        else:
            before = group < own
            unit(1, group, 0, None)
            unit(jnp.where(before, 0, 1), group, jnp.where(before, 0, 1), None)

    for _, block, source, targets in gather_plan():
        arrive(source, block)
        for target in targets:
            send(source, block, target)
        key = source[:2]
        waiting[key] -= 1
        if waiting[key] == 0:
            attend(*key)
    for copy in started:
        copy.wait_send()
    for which in range(2):
        total = jnp.sum(l[which], axis=1, keepdims=True)
        heads = (acc[which] / total).astype(jnp.bfloat16)
        for h in range(7):
            o[which, :, pl.ds(h * HD, HD)] = heads[h * BLOCK : (h + 1) * BLOCK]


def attend(q, kv):
    sends = 10 + sum(len(entry[3]) for entry in gather_plan())
    vmem = pl.BlockSpec(memory_space=pltpu.VMEM)
    return pl.pallas_call(
        attend_kernel,
        out_shape=jax.ShapeDtypeStruct((2, BLOCK, 7 * HD), jnp.bfloat16),
        in_specs=[vmem, vmem],
        out_specs=vmem,
        scratch_shapes=[
            pltpu.VMEM((32, 2, 2, BLOCK, HD), jnp.bfloat16),
            pltpu.VMEM((2, 7 * BLOCK, HD), jnp.float32),
            pltpu.VMEM((2, 7 * BLOCK, HD), jnp.float32),
            pltpu.VMEM((2, 7 * BLOCK, HD), jnp.float32),
            pltpu.SemaphoreType.DMA((sends,)),
            pltpu.SemaphoreType.DMA((32, 2)),
        ],
        compiler_params=pltpu.CompilerParams(
            collective_id=2, has_side_effects=True, vmem_limit_bytes=40 << 20
        ),
    )(q, kv)


def solution(mesh):
    placed = (
        P("seq", "head"),
        P(),
        P(),
        P(None, "head"),
        P(None, "head"),
        P(None, "head"),
        P("head"),
        P("head"),
        P("head"),
        P("head", None),
    )
    return jax.shard_map(
        on_device, mesh=mesh, in_specs=placed, out_specs=P(("seq", "head"), None), check_vma=False
    )
```

```python
import functools
import math

import jax
import jax.numpy as jnp
from jax import lax
from jax.experimental import pallas as pl
from jax.experimental.pallas import tpu as pltpu
from jax.sharding import PartitionSpec as P

HD = 128
HEADS = 7
FT = 16
FR_DEV = 16
HALF = FR_DEV // 2
SEQ = 32
TOK_DEV = 256
BLOCK = 128
QUARTER = 64
MODEL = 3584
PART = MODEL // 4
MESH = pl.DeviceIdType.MESH
NEG = -1e30
EXP_SCALE = math.log2(math.e) / math.sqrt(HD)
VMEM = pl.BlockSpec(memory_space=pltpu.VMEM)
SMEM = pl.BlockSpec(memory_space=pltpu.SMEM)
ANY = pl.BlockSpec(memory_space=pl.ANY)
CHUNK = 512
CHUNKS = MODEL // CHUNK


def remote(src, dst, send_sem, recv_sem, seq, head):
    return pltpu.make_async_remote_copy(
        src_ref=src,
        dst_ref=dst,
        send_sem=send_sem,
        recv_sem=recv_sem,
        device_id=(seq, head),
        device_id_type=MESH,
    )


def greet(barrier, seq, head):
    pl.semaphore_signal(barrier, inc=1, device_id=(seq, head), device_id_type=MESH)


def project_kernel(
    source_ref,
    visual,
    gain,
    q_bias,
    k_bias,
    v_bias,
    inverse,
    w_query_hbm,
    w_key_hbm,
    w_value_hbm,
    q_out,
    kv_out,
    send,
    recv,
    feat,
    normed,
    w_query,
    w_kv,
    cosine,
    sine,
    weight_sem,
    route_send,
    route_recv,
    near_send,
    near_recv,
    far_send,
    far_recv,
    pass_send,
    pass_recv,
):
    me = lax.axis_index("seq")
    head = lax.axis_index("head")
    sibling = head + 1 - 2 * (head % 2)
    pair = (head + 2) % 4
    cross = (sibling + 2) % 4

    loads = [
        pltpu.make_async_copy(w_key_hbm, w_kv.at[:, pl.ds(0, HD)], weight_sem.at[0]),
        pltpu.make_async_copy(w_value_hbm, w_kv.at[:, pl.ds(HD, HD)], weight_sem.at[1]),
        pltpu.make_async_copy(w_query_hbm, w_query, weight_sem.at[2]),
    ]
    for load in loads:
        load.start()

    barrier = pltpu.get_barrier_semaphore()

    def greet_seq(j, carry):
        greet(barrier, (me + j) % SEQ, head)
        return carry

    lax.fori_loop(1, SEQ, greet_seq, 0)
    greet(barrier, me, sibling)
    greet(barrier, me, pair)

    def frame_of(device, place):
        if place < HALF:
            return device * HALF + place
        return (2 * SEQ - 1 - device) * HALF + place - HALF

    def pick(device, carry):
        slot = jnp.int32(0)
        for place in range(FR_DEV):
            value = source_ref[frame_of(device, place)]
            slot += jnp.where(
                lax.shift_right_logical(value, 4) == me, jnp.bitwise_and(value, 15), 0
            )
        send[device] = visual[slot]
        return carry

    lax.fori_loop(0, SEQ, pick, 0)
    pl.semaphore_wait(barrier, SEQ + 1)

    def route(j):
        target = (me + j) % SEQ
        return remote(
            send.at[target],
            recv.at[me],
            route_send.at[target],
            route_recv.at[me],
            target,
            head,
        )

    def arrival(j):
        source = (me + j) % SEQ
        return remote(
            send.at[source],
            recv.at[source],
            route_send.at[source],
            route_recv.at[source],
            source,
            head,
        )

    def start_route(j, carry):
        route(j).start()
        return carry

    lax.fori_loop(1, SEQ, start_route, 0)
    recv[me] = send[me]

    for block in range(2):
        first = (me if block == 0 else 2 * SEQ - 1 - me) * BLOCK
        position = first + lax.broadcasted_iota(jnp.int32, (BLOCK, HD), 0)
        angle = position.astype(jnp.float32) * inverse[...]
        rows = pl.ds(block * BLOCK, BLOCK)
        cosine[rows, :] = jnp.cos(angle)
        lane = lax.broadcasted_iota(jnp.int32, (BLOCK, HD), 1)
        turned = jnp.sin(angle)
        sine[rows, :] = jnp.where(lane < HD // 2, -turned, turned)

    def end_route(j, carry):
        arrival(j).wait_recv()
        return carry

    lax.fori_loop(1, SEQ, end_route, 0)

    def part_copy(part, piece, sends, recvs, to):
        rows = pl.ds(piece * QUARTER, QUARTER)
        return remote(
            feat.at[part, rows, :],
            feat.at[part, rows, :],
            sends.at[piece],
            recvs.at[piece],
            me,
            to,
        )

    for piece in range(4):
        for place in range(4 * piece, 4 * piece + 4):
            source = lax.shift_right_logical(source_ref[frame_of(me, place)], 4)
            feat[head, pl.ds(place * FT, FT), :] = recv[source]
        part_copy(head, piece, far_send, far_recv, pair).start()
        part_copy(head, piece, near_send, near_recv, sibling).start()

    def norm_piece(piece):
        def rows_of(step, carry):
            rows = pl.ds(pl.multiple_of(piece * QUARTER + step * 16, 16), 16)
            total = jnp.zeros((16, 1), jnp.float32)
            for part in range(4):
                value = feat[part, rows, :].astype(jnp.float32)
                total += jnp.sum(value * value, axis=1, keepdims=True)
            factor = lax.rsqrt(total * (1.0 / MODEL) + 1e-06)
            for part in range(4):
                columns = pl.ds(part * PART, PART)
                value = feat[part, rows, :].astype(jnp.float32)
                scaled = value * factor * gain[:, columns].astype(jnp.float32)
                normed[rows, columns] = scaled.astype(jnp.bfloat16)
            return carry

        lax.fori_loop(0, QUARTER // 16, rows_of, 0)

    for piece in range(4):
        part_copy(pair, piece, far_send, far_recv, pair).wait_recv()
        part_copy(pair, piece, pass_send, pass_recv, sibling).start()
        part_copy(sibling, piece, near_send, near_recv, sibling).wait_recv()
        if piece > 0:
            part_copy(cross, piece - 1, pass_send, pass_recv, sibling).wait_recv()
            norm_piece(piece - 1)
    part_copy(cross, 3, pass_send, pass_recv, sibling).wait_recv()
    norm_piece(3)

    def rope(value, rows):
        return (value * cosine[rows, :] + pltpu.roll(value, HD // 2, 1) * sine[rows, :]).astype(
            jnp.bfloat16
        )

    loads[0].wait()
    loads[1].wait()
    both = jnp.dot(normed[...], w_kv[...], preferred_element_type=jnp.float32)
    for block in range(2):
        rows = pl.ds(block * BLOCK, BLOCK)
        part = both[block * BLOCK : (block + 1) * BLOCK]
        kv_out[block, 0] = rope(part[:, :HD] + k_bias[...].astype(jnp.float32), rows)
        kv_out[block, 1] = (part[:, HD:] + v_bias[...].astype(jnp.float32)).astype(jnp.bfloat16)
    loads[2].wait()
    for first in range(0, HEADS, 2):
        count = min(2, HEADS - first)
        columns = pl.ds(first * HD, count * HD)
        value = jnp.dot(normed[...], w_query[:, columns], preferred_element_type=jnp.float32)
        value = value + q_bias[:, columns].astype(jnp.float32)
        for h in range(count):
            for block in range(2):
                rows = pl.ds(block * BLOCK, BLOCK)
                one = value[block * BLOCK : (block + 1) * BLOCK, h * HD : (h + 1) * HD]
                q_out[block, pl.ds((first + h) * BLOCK, BLOCK), :] = rope(one, rows)

    def end_send(j, carry):
        route(j).wait_send()
        return carry

    lax.fori_loop(1, SEQ, end_send, 0)
    for piece in range(4):
        part_copy(head, piece, far_send, far_recv, pair).wait_send()
        part_copy(head, piece, near_send, near_recv, sibling).wait_send()
        part_copy(pair, piece, pass_send, pass_recv, sibling).wait_send()


def project(visual, frame_source, gain, w_query, w_key, w_value, q_bias, k_bias, v_bias):
    inverse = 1000000.0 ** (-(jnp.arange(HD // 2, dtype=jnp.float32) * 2.0) / HD)
    inverse = jnp.concatenate([inverse, inverse])[None]
    return pl.pallas_call(
        project_kernel,
        out_shape=(
            jax.ShapeDtypeStruct((2, HEADS * BLOCK, HD), jnp.bfloat16),
            jax.ShapeDtypeStruct((2, 2, BLOCK, HD), jnp.bfloat16),
        ),
        in_specs=[SMEM] + [VMEM] * 6 + [ANY] * 3,
        out_specs=(VMEM, VMEM),
        scratch_shapes=[
            pltpu.VMEM((SEQ, FT, PART), jnp.bfloat16),
            pltpu.VMEM((SEQ, FT, PART), jnp.bfloat16),
            pltpu.VMEM((4, TOK_DEV, PART), jnp.bfloat16),
            pltpu.VMEM((TOK_DEV, MODEL), jnp.bfloat16),
            pltpu.VMEM((MODEL, PART), jnp.bfloat16),
            pltpu.VMEM((MODEL, 2 * HD), jnp.bfloat16),
            pltpu.VMEM((TOK_DEV, HD), jnp.float32),
            pltpu.VMEM((TOK_DEV, HD), jnp.float32),
            pltpu.SemaphoreType.DMA((3,)),
            pltpu.SemaphoreType.DMA((SEQ,)),
            pltpu.SemaphoreType.DMA((SEQ,)),
        ]
        + [pltpu.SemaphoreType.DMA((4,))] * 6,
        compiler_params=pltpu.CompilerParams(
            collective_id=1, has_side_effects=True, vmem_limit_bytes=40 << 20
        ),
    )(
        frame_source,
        visual.reshape(FR_DEV, FT, PART),
        gain[None],
        q_bias[None],
        k_bias[None],
        v_bias[None],
        inverse,
        w_query,
        w_key,
        w_value,
    )


def coordinates():
    me = lax.axis_index("seq")
    return me, me // 16, (me // 4) % 4, me % 4


def near(dz, dx, dy):
    _, z, x, y = coordinates()
    return ((z + dz) % 2) * 16 + ((x + dx) % 4) * 4 + (y + dy) % 4


def gather_plan():
    plan = []
    for block in range(2):
        for dz in range(2):
            for dx in range(4):
                for dy in range(4):
                    if dz == dx == dy == 0:
                        continue
                    first, last = (dx, dy) if block == 0 else (dy, dx)
                    depth = dz + min(first, 4 - first) + min(last, 4 - last)
                    sends = []
                    if last == 0:
                        if first == 0:
                            sends += [(0, 1), (0, 3)]
                        if (first == 3 and dz == 0) or (first == 1 and dz == 1):
                            sends += [(0, 4 - first)]
                        sends += [(1, 1), (1, 3)]
                    elif (last == 3 and dz == 0) or (last == 1 and dz == 1):
                        sends += [(1, 4 - last)]
                    targets = []
                    for which, step in sends:
                        along_x = (which == 0) == (block == 0)
                        targets.append((0, step, 0) if along_x else (0, 0, step))
                    plan.append((depth, block, (dz, dx, dy), targets))
    plan.sort(key=lambda entry: (entry[0], entry[2][0], entry[2][1] == 2, entry[2][2] == 2))
    return plan


def attend_unit(q, buf, m, l, acc, which, group, block, keep):
    keys = buf[pl.ds(group * 4, 4), block, 0].reshape(4 * BLOCK, HD)
    vals = buf[pl.ds(group * 4, 4), block, 1].reshape(4 * BLOCK, HD)
    s = lax.dot_general(
        q[which], keys, (((1,), (1,)), ((), ())), preferred_element_type=jnp.float32
    )
    if keep is not None:
        s = jnp.where(keep, s, NEG)
    old = m[which]
    new = jnp.maximum(old, jnp.max(s, axis=1, keepdims=True))
    fade = jnp.exp2((old - new) * EXP_SCALE)
    p = jnp.exp2((s - jnp.concatenate([new] * 4, axis=1)) * EXP_SCALE)
    parts = p[:, :128] + p[:, 128:256] + p[:, 256:384] + p[:, 384:]
    l[which] = l[which] * fade + parts
    acc[which] = acc[which] * fade + jnp.dot(
        p.astype(jnp.bfloat16), vals, preferred_element_type=jnp.float32
    )
    m[which] = new


def attend_kernel(q, kv, o, buf, m, l, acc, send_sem, recv_sem):
    me, z, x, y = coordinates()
    head = lax.axis_index("head")
    own = me // 4
    partners = [(1, 0, 0), (0, 1, 0), (0, 3, 0), (0, 0, 1), (0, 0, 3)]
    barrier = pltpu.get_barrier_semaphore()
    for partner in partners:
        pl.semaphore_signal(
            barrier, inc=1, device_id=(near(*partner), head), device_id_type=MESH
        )
    buf[me] = kv[...]
    m[...] = jnp.full_like(m, NEG)
    l[...] = jnp.zeros_like(l)
    acc[...] = jnp.zeros_like(acc)
    pl.semaphore_wait(barrier, len(partners))

    started = []

    def send(source, block, target):
        index = near(*source)
        copy = pltpu.make_async_remote_copy(
            src_ref=buf.at[index, block],
            dst_ref=buf.at[index, block],
            send_sem=send_sem.at[len(started)],
            recv_sem=recv_sem.at[index, block],
            device_id=(near(*target), head),
            device_id_type=MESH,
        )
        copy.start()
        started.append(copy)

    def arrive(source, block):
        index = near(*source)
        pltpu.make_async_remote_copy(
            src_ref=buf.at[index, block],
            dst_ref=buf.at[index, block],
            send_sem=send_sem.at[0],
            recv_sem=recv_sem.at[index, block],
            device_id=(near(1, 0, 0), head),
            device_id_type=MESH,
        ).wait_recv()

    for block in range(2):
        send((0, 0, 0), block, (1, 0, 0))
    for block in range(2):
        for partner in partners[1:]:
            send((0, 0, 0), block, partner)

    waiting = {}
    for dz in range(2):
        for dx in range(4):
            waiting[dz, dx] = 8 if (dz, dx) != (0, 0) else 6

    def attend(dz, dx):
        group = near(dz, dx, 0) // 4
        unit = functools.partial(attend_unit, q, buf, m, l, acc)
        if (dz, dx) == (0, 0):
            row = lax.broadcasted_iota(jnp.int32, (7, BLOCK, 4 * BLOCK), 1)
            row = row.reshape(7 * BLOCK, 4 * BLOCK) + y * BLOCK
            column = lax.broadcasted_iota(jnp.int32, (7 * BLOCK, 4 * BLOCK), 1)
            unit(0, group, 0, column <= row)
            unit(1, group, 0, None)
            later = column % BLOCK - (column // BLOCK) * BLOCK
            unit(1, group, 1, later <= row - 2 * y * BLOCK)
        else:
            before = group < own
            unit(1, group, 0, None)
            unit(jnp.where(before, 0, 1), group, jnp.where(before, 0, 1), None)

    for _, block, source, targets in gather_plan():
        arrive(source, block)
        for target in targets:
            send(source, block, target)
        key = source[:2]
        waiting[key] -= 1
        if waiting[key] == 0:
            attend(*key)
    for copy in started:
        copy.wait_send()
    for which in range(2):
        total = jnp.sum(l[which], axis=1, keepdims=True)
        heads = (acc[which] / total).astype(jnp.bfloat16)
        for h in range(7):
            o[which, :, pl.ds(h * HD, HD)] = heads[h * BLOCK : (h + 1) * BLOCK]


def attend(q, kv):
    sends = 10 + sum(len(entry[3]) for entry in gather_plan())
    vmem = pl.BlockSpec(memory_space=pltpu.VMEM)
    return pl.pallas_call(
        attend_kernel,
        out_shape=jax.ShapeDtypeStruct((2, BLOCK, 7 * HD), jnp.bfloat16),
        in_specs=[vmem, vmem],
        out_specs=vmem,
        scratch_shapes=[
            pltpu.VMEM((32, 2, 2, BLOCK, HD), jnp.bfloat16),
            pltpu.VMEM((2, 7 * BLOCK, HD), jnp.float32),
            pltpu.VMEM((2, 7 * BLOCK, HD), jnp.float32),
            pltpu.VMEM((2, 7 * BLOCK, HD), jnp.float32),
            pltpu.SemaphoreType.DMA((sends,)),
            pltpu.SemaphoreType.DMA((32, 2)),
        ],
        compiler_params=pltpu.CompilerParams(
            collective_id=2, has_side_effects=True, vmem_limit_bytes=40 << 20
        ),
    )(q, kv)


def output_kernel(
    heads,
    w_hbm,
    out,
    rows,
    w,
    near_out,
    near_in,
    far_out,
    far_in,
    kept,
    weight_sem,
    near_send,
    near_recv,
    far_send,
    far_recv,
):
    me = lax.axis_index("seq")
    head = lax.axis_index("head")
    sibling = head + 1 - 2 * (head % 2)
    pair = (head + 2) % 4
    cross = (sibling + 2) % 4
    loads = []
    for j in range(CHUNKS):
        columns = pl.ds(j * CHUNK, CHUNK)
        loads.append(
            pltpu.make_async_copy(w_hbm.at[:, columns], w.at[j], weight_sem.at[j])
        )
        loads[j].start()
    barrier = pltpu.get_barrier_semaphore()
    greet(barrier, me, sibling)
    greet(barrier, me, pair)
    for place, owner in enumerate((cross, sibling, pair, head)):
        rows[pl.ds(place * QUARTER, QUARTER), :] = heads[
            pl.ds(pl.multiple_of(owner * QUARTER, QUARTER), QUARTER), :
        ]
    pl.semaphore_wait(barrier, 2)

    def near_copy(j):
        return remote(
            near_out.at[j], near_in.at[j], near_send.at[j], near_recv.at[j], me, sibling
        )

    def far_copy(j):
        return remote(far_out.at[j], far_in.at[j], far_send.at[j], far_recv.at[j], me, pair)

    def relay(j):
        near_copy(j).wait_recv()
        far_out[j] += near_in[j, pl.ds(0, QUARTER), :]
        far_copy(j).start()
        kept[j] += near_in[j, pl.ds(QUARTER, QUARTER), :]

    for j in range(CHUNKS):
        loads[j].wait()
        value = jnp.dot(rows[...], w[j], preferred_element_type=jnp.float32)
        near_out[j] = value[: 2 * QUARTER]
        near_copy(j).start()
        far_out[j] = value[2 * QUARTER : 3 * QUARTER]
        kept[j] = value[3 * QUARTER :]
        if j > 0:
            relay(j - 1)
    relay(CHUNKS - 1)
    for j in range(CHUNKS):
        far_copy(j).wait_recv()
        total = kept[j] + far_in[j]
        out[:, pl.ds(j * CHUNK, CHUNK)] = total.astype(jnp.bfloat16)
    for j in range(CHUNKS):
        near_copy(j).wait_send()
        far_copy(j).wait_send()


def project_out(heads, w_out):
    return pl.pallas_call(
        output_kernel,
        out_shape=jax.ShapeDtypeStruct((QUARTER, MODEL), jnp.bfloat16),
        in_specs=[VMEM, ANY],
        out_specs=VMEM,
        scratch_shapes=[
            pltpu.VMEM((TOK_DEV, PART), jnp.bfloat16),
            pltpu.VMEM((CHUNKS, PART, CHUNK), jnp.bfloat16),
            pltpu.VMEM((CHUNKS, 2 * QUARTER, CHUNK), jnp.float32),
            pltpu.VMEM((CHUNKS, 2 * QUARTER, CHUNK), jnp.float32),
            pltpu.VMEM((CHUNKS, QUARTER, CHUNK), jnp.float32),
            pltpu.VMEM((CHUNKS, QUARTER, CHUNK), jnp.float32),
            pltpu.VMEM((CHUNKS, QUARTER, CHUNK), jnp.float32),
        ]
        + [pltpu.SemaphoreType.DMA((CHUNKS,))] * 5,
        compiler_params=pltpu.CompilerParams(
            collective_id=3, has_side_effects=True, vmem_limit_bytes=40 << 20
        ),
    )(heads, w_out)


def on_device(
    visual, frame_source, input_norm_gain, w_query, w_key, w_value, q_bias, k_bias, v_bias, w_out
):
    q, kv = project(
        visual, frame_source, input_norm_gain, w_query, w_key, w_value, q_bias, k_bias, v_bias
    )
    heads = attend(q, kv).reshape(TOK_DEV, PART)
    return project_out(heads, w_out)


def solution(mesh):
    placed = (
        P("seq", "head"),
        P(),
        P(),
        P(None, "head"),
        P(None, "head"),
        P(None, "head"),
        P("head"),
        P("head"),
        P("head"),
        P("head", None),
    )
    return jax.shard_map(
        on_device, mesh=mesh, in_specs=placed, out_specs=P(("seq", "head"), None), check_vma=False
    )
```

```python
import functools
import math

import jax
import jax.numpy as jnp
from jax import lax
from jax.experimental import pallas as pl
from jax.experimental.pallas import tpu as pltpu
from jax.sharding import PartitionSpec as P

HD = 128
HEADS = 7
FT = 16
FR_DEV = 16
HALF = FR_DEV // 2
SEQ = 32
TOK_DEV = 256
BLOCK = 128
QUARTER = 64
MODEL = 3584
PART = MODEL // 4
MESH = pl.DeviceIdType.MESH
NEG = -1e30
EXP_SCALE = math.log2(math.e) / math.sqrt(HD)
VMEM = pl.BlockSpec(memory_space=pltpu.VMEM)
ANY = pl.BlockSpec(memory_space=pl.ANY)
CHUNK = 512
CHUNKS = MODEL // CHUNK


def remote(src, dst, send_sem, recv_sem, seq, head):
    return pltpu.make_async_remote_copy(
        src_ref=src,
        dst_ref=dst,
        send_sem=send_sem,
        recv_sem=recv_sem,
        device_id=(seq, head),
        device_id_type=MESH,
    )

HALF_CHUNK = CHUNK // 2
SMALL = MODEL + PART + 3 * HD

SCHEDULE = (
    12, 35, 16, 4, 33, 44, 36, 3, 1, 48, 8, 15, 13, 39, 47, 34,
    17, 20, 28, 19, 5, 37, 45, 7, 49, 52, 40, 2, 80, 9, 38, 64,
    51, 24, 60, 18, 72, 11, 21, 53, 43, 68, 46, 29, 14, 56, 67, 50,
    41, 23, 76, 55, 61, 31, 75, 25, 57, 63, 6, 65, 54, 22, 73, 42,
    27, 30, 69, 59, 62, 10, 26, 77, 71, 58, 79, 66, 74, 70, 78,
)


def coordinates():
    me = lax.axis_index("seq")
    return me, me // 16, (me // 4) % 4, me % 4


def near(dz, dx, dy):
    _, z, x, y = coordinates()
    return ((z + dz) % 2) * 16 + ((x + dx) % 4) * 4 + (y + dy) % 4


def gather_plan():
    plan = {}
    for block in range(2):
        for dz in range(2):
            for dx in range(4):
                for dy in range(4):
                    if dz == dx == dy == 0:
                        continue
                    first, last = (dx, dy) if block == 0 else (dy, dx)
                    sends = []
                    if last == 0:
                        if first == 0:
                            sends += [(0, 1), (0, 3)]
                        if (first == 3 and dz == 0) or (first == 1 and dz == 1):
                            sends += [(0, 4 - first)]
                        sends += [(1, 1), (1, 3)]
                    elif (last == 3 and dz == 0) or (last == 1 and dz == 1):
                        sends += [(1, 4 - last)]
                    targets = []
                    for which, step in sends:
                        along_x = (which == 0) == (block == 0)
                        targets.append((0, step, 0) if along_x else (0, 0, step))
                    plan[block, dz, dx, dy] = targets
    return plan


def attend_unit(q, buf, m, l, acc, which, group, block, keep):
    keys = buf[pl.ds(group * 4, 4), block, 0].reshape(4 * BLOCK, HD)
    vals = buf[pl.ds(group * 4, 4), block, 1].reshape(4 * BLOCK, HD)
    s = lax.dot_general(
        q[which], keys, (((1,), (1,)), ((), ())), preferred_element_type=jnp.float32
    )
    if keep is not None:
        s = jnp.where(keep, s, NEG)
    old = m[which]
    new = jnp.maximum(old, jnp.max(s, axis=1, keepdims=True))
    fade = jnp.exp2((old - new) * EXP_SCALE)
    p = jnp.exp2((s - jnp.concatenate([new] * 4, axis=1)) * EXP_SCALE)
    parts = p[:, :128] + p[:, 128:256] + p[:, 256:384] + p[:, 384:]
    l[which] = l[which] * fade + parts
    acc[which] = acc[which] * fade + jnp.dot(
        p.astype(jnp.bfloat16), vals, preferred_element_type=jnp.float32
    )
    m[which] = new


FIRST_SENDS = (
    (0, (0, 1, 0)),
    (0, (0, 3, 0)),
    (1, (0, 0, 1)),
    (1, (0, 0, 3)),
    (0, (1, 0, 0)),
    (1, (1, 0, 0)),
    (1, (0, 1, 0)),
    (1, (0, 3, 0)),
    (0, (0, 0, 1)),
    (0, (0, 0, 3)),
)


def greet(barrier, seq, head):
    pl.semaphore_signal(barrier, inc=1, device_id=(seq, head), device_id_type=MESH)


def scratch():
    copies = pltpu.SemaphoreType.DMA
    bf16 = jnp.bfloat16
    f32 = jnp.float32
    gather_sends = len(FIRST_SENDS) + sum(len(targets) for targets in gather_plan().values())
    state = pltpu.VMEM((2, HEADS * BLOCK, HD), f32)
    return dict(
        source_ref=pltpu.SMEM((SEQ * FR_DEV,), jnp.int32),
        visual=pltpu.VMEM((FR_DEV, FT, PART), bf16),
        small=pltpu.VMEM((1, SMALL), f32),
        send=pltpu.VMEM((SEQ, FT, PART), bf16),
        recv=pltpu.VMEM((SEQ, FT, PART), bf16),
        feat=pltpu.VMEM((4, TOK_DEV, PART), bf16),
        normed=pltpu.VMEM((TOK_DEV, MODEL), bf16),
        w_query=pltpu.VMEM((MODEL, PART), bf16),
        w_kv=pltpu.VMEM((MODEL, 2 * HD), bf16),
        w_out=pltpu.VMEM((CHUNKS, PART, CHUNK), bf16),
        cosine=pltpu.VMEM((TOK_DEV, HD), f32),
        sine=pltpu.VMEM((TOK_DEV, HD), f32),
        q=pltpu.VMEM((2, HEADS * BLOCK, HD), bf16),
        buf=pltpu.VMEM((SEQ, 2, 2, BLOCK, HD), bf16),
        m=state,
        l=state,
        acc=state,
        heads=pltpu.VMEM((4, QUARTER, PART), bf16),
        rows=pltpu.VMEM((3 * QUARTER, PART), bf16),
        given=pltpu.VMEM((QUARTER, PART), bf16),
        near_out=pltpu.VMEM((CHUNKS, 3 * QUARTER, HALF_CHUNK), f32),
        near_in=pltpu.VMEM((CHUNKS, 3 * QUARTER, HALF_CHUNK), f32),
        extra_out=pltpu.VMEM((CHUNKS, QUARTER, HALF_CHUNK), f32),
        extra_in=pltpu.VMEM((CHUNKS, QUARTER, HALF_CHUNK), f32),
        far_out=pltpu.VMEM((2, CHUNKS, QUARTER, HALF_CHUNK), f32),
        far_in=pltpu.VMEM((CHUNKS, 2, QUARTER, HALF_CHUNK), f32),
        kept=pltpu.VMEM((CHUNKS, QUARTER, CHUNK), f32),
        load_sem=copies((6,)),
        out_load_sem=copies((CHUNKS,)),
        route_send=copies((SEQ,)),
        route_recv=copies((SEQ,)),
        near_send=copies((4,)),
        near_recv=copies((4,)),
        far_send=copies((4,)),
        far_recv=copies((4,)),
        pass_send=copies((4,)),
        pass_recv=copies((4,)),
        gather_send=copies((gather_sends,)),
        gather_recv=copies((SEQ, 2)),
        given_sem=copies((2,)),
        near_sum_send=copies((CHUNKS,)),
        near_sum_recv=copies((CHUNKS,)),
        extra_send=copies((CHUNKS,)),
        extra_recv=copies((CHUNKS,)),
        far_sum_send=copies((2, CHUNKS)),
        far_sum_recv=copies((CHUNKS, 2)),
    )


class Refs:
    def __init__(self, **refs):
        self.__dict__.update(refs)


def places():
    me = lax.axis_index("seq")
    head = lax.axis_index("head")
    sibling = head + 1 - 2 * (head % 2)
    return me, head, sibling, (head + 2) % 4, (sibling + 2) % 4


def frame_of(device, place):
    if place < HALF:
        return device * HALF + place
    return (2 * SEQ - 1 - device) * HALF + place - HALF


def route_frames(r):
    me, head, _, _, _ = places()

    def pick(device, carry):
        slot = jnp.int32(0)
        for place in range(FR_DEV):
            value = r.source_ref[frame_of(device, place)]
            slot += jnp.where(
                lax.shift_right_logical(value, 4) == me, jnp.bitwise_and(value, 15), 0
            )
        r.send[device] = r.visual[slot]
        return carry

    lax.fori_loop(0, SEQ, pick, 0)
    pl.semaphore_wait(pltpu.get_barrier_semaphore(), SEQ + 4)

    def route(j):
        target = (me + j) % SEQ
        return remote(
            r.send.at[target],
            r.recv.at[me],
            r.route_send.at[target],
            r.route_recv.at[me],
            target,
            head,
        )

    def arrival(j):
        source = (me + j) % SEQ
        return remote(
            r.send.at[source],
            r.recv.at[source],
            r.route_send.at[source],
            r.route_recv.at[source],
            source,
            head,
        )

    def start_route(j, carry):
        route(j).start()
        return carry

    lax.fori_loop(1, SEQ, start_route, 0)
    r.recv[me] = r.send[me]
    angles(r)

    def end_route(j, carry):
        arrival(j).wait_recv()
        return carry

    lax.fori_loop(1, SEQ, end_route, 0)

    def end_send(j, carry):
        route(j).wait_send()
        return carry

    return lambda: lax.fori_loop(1, SEQ, end_send, 0)


def angles(r):
    me = lax.axis_index("seq")
    inverse = r.small[:, pl.ds(MODEL + PART + 2 * HD, HD)]
    for block in range(2):
        first = (me if block == 0 else 2 * SEQ - 1 - me) * BLOCK
        position = first + lax.broadcasted_iota(jnp.int32, (BLOCK, HD), 0)
        angle = position.astype(jnp.float32) * inverse
        rows = pl.ds(block * BLOCK, BLOCK)
        r.cosine[rows, :] = jnp.cos(angle)
        lane = lax.broadcasted_iota(jnp.int32, (BLOCK, HD), 1)
        turned = jnp.sin(angle)
        r.sine[rows, :] = jnp.where(lane < HD // 2, -turned, turned)


def gather_features(r):
    me, head, sibling, pair, cross = places()

    def part_copy(part, piece, sends, recvs, to):
        rows = pl.ds(piece * QUARTER, QUARTER)
        block = r.feat.at[part, rows, :]
        return remote(block, block, sends.at[piece], recvs.at[piece], me, to)

    def far(part, piece):
        return part_copy(part, piece, r.far_send, r.far_recv, pair)

    def near_part(part, piece):
        return part_copy(part, piece, r.near_send, r.near_recv, sibling)

    def passed(part, piece):
        return part_copy(part, piece, r.pass_send, r.pass_recv, sibling)

    for piece in range(4):
        for place in range(4 * piece, 4 * piece + 4):
            source = lax.shift_right_logical(r.source_ref[frame_of(me, place)], 4)
            r.feat[head, pl.ds(place * FT, FT), :] = r.recv[source]
        far(head, piece).start()
        near_part(head, piece).start()

    def norm_piece(piece):
        def rows_of(step, carry):
            rows = pl.ds(pl.multiple_of(piece * QUARTER + step * 16, 16), 16)
            total = jnp.zeros((16, 1), jnp.float32)
            for part in range(4):
                value = r.feat[part, rows, :].astype(jnp.float32)
                total += jnp.sum(value * value, axis=1, keepdims=True)
            factor = lax.rsqrt(total * (1.0 / MODEL) + 1e-06)
            for part in range(4):
                columns = pl.ds(part * PART, PART)
                value = r.feat[part, rows, :].astype(jnp.float32)
                scaled = value * factor * r.small[:, columns]
                r.normed[rows, columns] = scaled.astype(jnp.bfloat16)
            return carry

        lax.fori_loop(0, QUARTER // 16, rows_of, 0)

    for piece in range(4):
        far(pair, piece).wait_recv()
        passed(pair, piece).start()
        near_part(sibling, piece).wait_recv()
        if piece > 0:
            passed(cross, piece - 1).wait_recv()
            norm_piece(piece - 1)
    passed(cross, 3).wait_recv()
    norm_piece(3)

    def finish():
        for piece in range(4):
            far(head, piece).wait_send()
            near_part(head, piece).wait_send()
            passed(pair, piece).wait_send()

    return finish


def rope(r, value, block):
    rows = pl.ds(block * BLOCK, BLOCK)
    turned = pltpu.roll(value, HD // 2, 1) * r.sine[rows, :]
    return (value * r.cosine[rows, :] + turned).astype(jnp.bfloat16)


def project_keys(r):
    me = lax.axis_index("seq")
    both = jnp.dot(r.normed[...], r.w_kv[...], preferred_element_type=jnp.float32)
    both = both + r.small[:, pl.ds(MODEL + PART, 2 * HD)]
    for block in range(2):
        part = both[block * BLOCK : (block + 1) * BLOCK]
        r.buf[me, block, 0] = rope(r, part[:, :HD], block)
        r.buf[me, block, 1] = part[:, HD:].astype(jnp.bfloat16)


def project_queries(r):
    for first in range(0, HEADS, 2):
        count = min(2, HEADS - first)
        columns = pl.ds(first * HD, count * HD)
        value = jnp.dot(r.normed[...], r.w_query[:, columns], preferred_element_type=jnp.float32)
        value = value + r.small[:, pl.ds(MODEL + first * HD, count * HD)]
        for h in range(count):
            for block in range(2):
                one = value[block * BLOCK : (block + 1) * BLOCK, h * HD : (h + 1) * HD]
                r.q[block, pl.ds((first + h) * BLOCK, BLOCK), :] = rope(r, one, block)


def gather_attend(r):
    me, _, _, y = coordinates()
    head = lax.axis_index("head")
    own = me // 4
    started = []

    def copy_of(source, block, target, send_sem):
        index = near(*source)
        one = r.buf.at[index, block]
        return remote(one, one, send_sem, r.gather_recv.at[index, block], near(*target), head)

    def send(source, block, target):
        started.append(copy_of(source, block, target, r.gather_send.at[len(started)]))
        started[-1].start()

    def attend(kind, dz, dx):
        group = near(dz, dx, 0) // 4
        unit = functools.partial(attend_unit, r.q, r.buf, r.m, r.l, r.acc)
        if (dz, dx) != (0, 0):
            which = jnp.where(group < own, 0, 1)
            if kind == 0:
                unit(1, group, 0, None)
            else:
                unit(which, group, which, None)
            return
        row = lax.broadcasted_iota(jnp.int32, (HEADS, BLOCK, 4 * BLOCK), 1)
        row = row.reshape(HEADS * BLOCK, 4 * BLOCK) + y * BLOCK
        column = lax.broadcasted_iota(jnp.int32, (HEADS * BLOCK, 4 * BLOCK), 1)
        if kind == 0:
            unit(1, group, 0, None)
        elif kind == 1:
            later = column % BLOCK - (column // BLOCK) * BLOCK
            unit(1, group, 1, later <= row - 2 * y * BLOCK)
        else:
            unit(0, group, 0, column <= row)

    for block, target in FIRST_SENDS:
        send((0, 0, 0), block, target)
    project_queries(r)
    plan = gather_plan()
    for code in SCHEDULE:
        if code >= 64:
            attend((code - 64) // 8, (code % 8) // 4, code % 4)
            continue
        block, source = code // 32, ((code // 16) % 2, (code // 4) % 4, code % 4)
        copy_of(source, block, (1, 0, 0), r.gather_send.at[0]).wait_recv()
        for target in plan[(block, *source)]:
            send(source, block, target)

    def finish():
        for copy in started:
            copy.wait_send()

    return finish


def output(r, out):
    me, head, sibling, pair, _ = places()
    other = near(1, 0, 0)
    core = head % 2
    theirs = 2 * ((head // 2 + 1) % 2)
    for which in range(2):
        total = jnp.sum(r.l[which], axis=1, keepdims=True)
        value = (r.acc[which] / total).astype(jnp.bfloat16)
        for h in range(HEADS):
            for half in range(2):
                first = h * BLOCK + half * QUARTER
                r.heads[2 * which + half, :, pl.ds(h * HD, HD)] = value[first : first + QUARTER]
    gift = remote(
        r.heads.at[theirs + 1], r.given, r.given_sem.at[0], r.given_sem.at[1], other, head
    )
    gift.start()
    for place, quarter in enumerate((theirs, sibling, head)):
        r.rows[pl.ds(place * QUARTER, QUARTER), :] = r.heads[quarter]

    def near_copy(j):
        return remote(
            r.near_out.at[j],
            r.near_in.at[j],
            r.near_sum_send.at[j],
            r.near_sum_recv.at[j],
            me,
            sibling,
        )

    def extra_copy(j):
        return remote(
            r.extra_out.at[j],
            r.extra_in.at[j],
            r.extra_send.at[j],
            r.extra_recv.at[j],
            me,
            sibling,
        )

    def far_copy(which, j):
        return remote(
            r.far_out.at[which, j],
            r.far_in.at[j, core],
            r.far_sum_send.at[which, j],
            r.far_sum_recv.at[j, core],
            other if which else me,
            theirs + which,
        )

    def split(value):
        left, right = value[:, :HALF_CHUNK], value[:, HALF_CHUNK:]
        return jnp.where(core == 0, left, right), jnp.where(core == 0, right, left)

    def relay(j):
        near_copy(j).wait_recv()
        r.far_out[0, j] += r.near_in[j, pl.ds(0, QUARTER), :]
        far_copy(0, j).start()
        for half in range(2):
            r.kept[j, :, pl.ds(half * HALF_CHUNK, HALF_CHUNK)] += r.near_in[
                j, pl.ds((half + 1) * QUARTER, QUARTER), :
            ]

    def relay_extra(j):
        extra_copy(j).wait_recv()
        r.far_out[1, j] += r.extra_in[j]
        far_copy(1, j).start()

    for j in range(CHUNKS):
        value = jnp.dot(r.rows[...], r.w_out[j], preferred_element_type=jnp.float32)
        mine, handed = split(value[:QUARTER])
        r.near_out[j, pl.ds(0, QUARTER), :] = handed
        for half in range(2):
            r.near_out[j, pl.ds((half + 1) * QUARTER, QUARTER), :] = value[
                QUARTER : 2 * QUARTER, half * HALF_CHUNK : (half + 1) * HALF_CHUNK
            ]
        near_copy(j).start()
        r.far_out[0, j] = mine
        r.kept[j] = value[2 * QUARTER :]
        if j > 0:
            relay(j - 1)
    relay(CHUNKS - 1)
    gift.wait()
    for j in range(CHUNKS):
        value = jnp.dot(r.given[...], r.w_out[j], preferred_element_type=jnp.float32)
        mine, handed = split(value)
        r.extra_out[j] = handed
        extra_copy(j).start()
        r.far_out[1, j] = mine
        if j > 0:
            relay_extra(j - 1)
    relay_extra(CHUNKS - 1)
    for j in range(CHUNKS):
        for half in range(2):
            remote(
                r.far_out.at[0, j],
                r.far_in.at[j, half],
                r.far_sum_send.at[0, j],
                r.far_sum_recv.at[j, half],
                me,
                pair,
            ).wait_recv()
            columns = pl.ds(half * HALF_CHUNK, HALF_CHUNK)
            total = r.kept[j, :, columns] + r.far_in[j, half]
            out[:, pl.ds(j * CHUNK + half * HALF_CHUNK, HALF_CHUNK)] = total.astype(jnp.bfloat16)
    for j in range(CHUNKS):
        near_copy(j).wait_send()
        extra_copy(j).wait_send()
        for which in range(2):
            far_copy(which, j).wait_send()


INPUTS = ("source_hbm", "visual_hbm", "small_hbm", "query_hbm", "key_hbm", "value_hbm", "out_hbm")


def kernel(*refs):
    names = INPUTS + ("out",) + tuple(scratch())
    r = Refs(**dict(zip(names, refs)))
    me, head, sibling, pair, cross = places()
    barrier = pltpu.get_barrier_semaphore()

    def greet_seq(j, carry):
        greet(barrier, (me + j) % SEQ, head)
        return carry

    lax.fori_loop(1, SEQ, greet_seq, 0)
    for each in (sibling, pair, cross):
        greet(barrier, me, each)
    for each in (pair, cross):
        greet(barrier, near(1, 0, 0), each)

    pairs = (
        (r.source_hbm, r.source_ref),
        (r.visual_hbm, r.visual),
        (r.small_hbm, r.small),
        (r.key_hbm, r.w_kv.at[:, pl.ds(0, HD)]),
        (r.value_hbm, r.w_kv.at[:, pl.ds(HD, HD)]),
        (r.query_hbm, r.w_query),
    )
    loads = [pltpu.make_async_copy(a, b, r.load_sem.at[i]) for i, (a, b) in enumerate(pairs)]
    for j in range(CHUNKS):
        block = r.out_hbm.at[:, pl.ds(j * CHUNK, CHUNK)]
        loads.append(pltpu.make_async_copy(block, r.w_out.at[j], r.out_load_sem.at[j]))
    for load in loads:
        load.start()
    r.m[...] = jnp.full_like(r.m, NEG)
    r.l[...] = jnp.zeros_like(r.l)
    r.acc[...] = jnp.zeros_like(r.acc)
    for load in loads[:3]:
        load.wait()
    endings = [route_frames(r), gather_features(r)]
    for load in loads[3:]:
        load.wait()
    project_keys(r)
    endings.append(gather_attend(r))
    output(r, r.out)
    for ending in endings:
        ending()


def on_device(
    visual, frame_source, input_norm_gain, w_query, w_key, w_value, q_bias, k_bias, v_bias, w_out
):
    inverse = 1000000.0 ** (-(jnp.arange(HD // 2, dtype=jnp.float32) * 2.0) / HD)
    small = [each.astype(jnp.float32) for each in (input_norm_gain, q_bias, k_bias, v_bias)]
    small = jnp.concatenate(small + [inverse, inverse])[None]
    return pl.pallas_call(
        kernel,
        out_shape=jax.ShapeDtypeStruct((QUARTER, MODEL), jnp.bfloat16),
        in_specs=[ANY] * len(INPUTS),
        out_specs=VMEM,
        scratch_shapes=list(scratch().values()),
        compiler_params=pltpu.CompilerParams(
            collective_id=1, has_side_effects=True, vmem_limit_bytes=60 << 20
        ),
    )(
        frame_source,
        visual.reshape(FR_DEV, FT, PART),
        small,
        w_query,
        w_key,
        w_value,
        w_out,
    )


def solution(mesh):
    placed = (
        P("seq", "head"),
        P(),
        P(),
        P(None, "head"),
        P(None, "head"),
        P(None, "head"),
        P("head"),
        P("head"),
        P("head"),
        P("head", None),
    )
    return jax.shard_map(
        on_device, mesh=mesh, in_specs=placed, out_specs=P(("seq", "head"), None), check_vma=False
    )
```

```python
import functools
import math

import jax
import jax.numpy as jnp
import numpy as np
from jax import lax
from jax.experimental import pallas as pl
from jax.experimental.pallas import tpu as pltpu
from jax.sharding import PartitionSpec as P

HD = 128
HEADS = 7
FT = 16
FR_DEV = 16
HALF = FR_DEV // 2
SEQ = 32
TOK_DEV = 256
BLOCK = 128
QUARTER = 64
MODEL = 3584
PART = MODEL // 4
MESH = pl.DeviceIdType.MESH
NEG = -1e30
EXP_SCALE = math.log2(math.e) / math.sqrt(HD)
VMEM = pl.BlockSpec(memory_space=pltpu.VMEM)
ANY = pl.BlockSpec(memory_space=pl.ANY)
CHUNK = 512
CHUNKS = MODEL // CHUNK


def remote(src, dst, send_sem, recv_sem, seq, head):
    return pltpu.make_async_remote_copy(
        src_ref=src,
        dst_ref=dst,
        send_sem=send_sem,
        recv_sem=recv_sem,
        device_id=(seq, head),
        device_id_type=MESH,
    )

HALF_CHUNK = CHUNK // 2
PIECES = ((0, 512), (512, 384))

SCHEDULE = (
    12, 35, 16, 4, 33, 44, 36, 3, 1, 48, 8, 15, 13, 39, 47, 34,
    17, 20, 28, 19, 5, 37, 45, 7, 49, 52, 40, 2, 80, 9, 38, 64,
    51, 24, 60, 18, 72, 11, 21, 53, 43, 68, 46, 29, 14, 56, 67, 50,
    41, 23, 76, 55, 61, 31, 75, 25, 57, 63, 6, 65, 54, 22, 73, 42,
    27, 30, 69, 59, 62, 10, 26, 77, 71, 58, 79, 66, 74, 70, 78,
)


def coordinates():
    me = lax.axis_index("seq")
    return me, me // 16, (me // 4) % 4, me % 4


def near(dz, dx, dy):
    _, z, x, y = coordinates()
    return ((z + dz) % 2) * 16 + ((x + dx) % 4) * 4 + (y + dy) % 4


def gather_plan():
    plan = {}
    for block in range(2):
        for dz in range(2):
            for dx in range(4):
                for dy in range(4):
                    if dz == dx == dy == 0:
                        continue
                    first, last = (dx, dy) if block == 0 else (dy, dx)
                    sends = []
                    if last == 0:
                        if first == 0:
                            sends += [(0, 1), (0, 3)]
                        if (first == 3 and dz == 0) or (first == 1 and dz == 1):
                            sends += [(0, 4 - first)]
                        sends += [(1, 1), (1, 3)]
                    elif (last == 3 and dz == 0) or (last == 1 and dz == 1):
                        sends += [(1, 4 - last)]
                    targets = []
                    for which, step in sends:
                        along_x = (which == 0) == (block == 0)
                        targets.append((0, step, 0) if along_x else (0, 0, step))
                    plan[block, dz, dx, dy] = targets
    return plan


def attend_unit(q, buf, m, l, acc, which, group, block, keep):
    keys = buf[pl.ds(group * 4, 4), block, 0].reshape(4 * BLOCK, HD)
    vals = buf[pl.ds(group * 4, 4), block, 1].reshape(4 * BLOCK, HD)
    s = lax.dot_general(
        q[which], keys, (((1,), (1,)), ((), ())), preferred_element_type=jnp.float32
    )
    if keep is not None:
        s = jnp.where(keep, s, NEG)
    old = m[which]
    new = jnp.maximum(old, jnp.max(s, axis=1, keepdims=True))
    fade = jnp.exp2((old - new) * EXP_SCALE)
    p = jnp.exp2((s - jnp.concatenate([new] * 4, axis=1)) * EXP_SCALE)
    parts = p[:, :128] + p[:, 128:256] + p[:, 256:384] + p[:, 384:]
    l[which] = l[which] * fade + parts
    acc[which] = acc[which] * fade + jnp.dot(
        p.astype(jnp.bfloat16), vals, preferred_element_type=jnp.float32
    )
    m[which] = new


FIRST_SENDS = (
    (0, (0, 1, 0)),
    (0, (0, 3, 0)),
    (1, (0, 0, 1)),
    (1, (0, 0, 3)),
    (0, (1, 0, 0)),
    (1, (1, 0, 0)),
    (1, (0, 1, 0)),
    (1, (0, 3, 0)),
    (0, (0, 0, 1)),
    (0, (0, 0, 3)),
)


def greet(barrier, seq, head):
    pl.semaphore_signal(barrier, inc=1, device_id=(seq, head), device_id_type=MESH)


def scratch():
    copies = pltpu.SemaphoreType.DMA
    bf16 = jnp.bfloat16
    f32 = jnp.float32
    gather_sends = len(FIRST_SENDS) + sum(len(targets) for targets in gather_plan().values())
    state = pltpu.VMEM((2, HEADS * BLOCK, HD), f32)
    return dict(
        source_ref=pltpu.SMEM((SEQ * FR_DEV,), jnp.int32),
        visual=pltpu.VMEM((FR_DEV, FT, PART), bf16),
        gain=pltpu.VMEM((MODEL,), bf16),
        q_bias=pltpu.VMEM((PART,), bf16),
        k_bias=pltpu.VMEM((HD,), bf16),
        v_bias=pltpu.VMEM((HD,), bf16),
        inverse=pltpu.VMEM((1, HD), f32),
        **{f"send{k}": pltpu.VMEM((SEQ, FT, w), bf16) for k, (_, w) in enumerate(PIECES)},
        **{f"recv{k}": pltpu.VMEM((SEQ, FT, w), bf16) for k, (_, w) in enumerate(PIECES)},
        **{f"feat{k}": pltpu.VMEM((4, TOK_DEV, w), bf16) for k, (_, w) in enumerate(PIECES)},
        squares=pltpu.VMEM((TOK_DEV, HD), f32),
        normed=pltpu.VMEM((TOK_DEV, MODEL), bf16),
        w_query=pltpu.VMEM((MODEL, PART), bf16),
        w_kv=pltpu.VMEM((MODEL, 2 * HD), bf16),
        w_out=pltpu.VMEM((CHUNKS, PART, CHUNK), bf16),
        cosine=pltpu.VMEM((TOK_DEV, HD), f32),
        sine=pltpu.VMEM((TOK_DEV, HD), f32),
        q=pltpu.VMEM((2, HEADS * BLOCK, HD), bf16),
        buf=pltpu.VMEM((SEQ, 2, 2, BLOCK, HD), bf16),
        m=state,
        l=state,
        acc=state,
        heads=pltpu.VMEM((4, QUARTER, PART), bf16),
        rows=pltpu.VMEM((3 * QUARTER, PART), bf16),
        given=pltpu.VMEM((QUARTER, PART), bf16),
        near_out=pltpu.VMEM((CHUNKS, 3 * QUARTER, HALF_CHUNK), f32),
        near_in=pltpu.VMEM((CHUNKS, 3 * QUARTER, HALF_CHUNK), f32),
        extra_out=pltpu.VMEM((CHUNKS, QUARTER, HALF_CHUNK), f32),
        extra_in=pltpu.VMEM((CHUNKS, QUARTER, HALF_CHUNK), f32),
        far_out=pltpu.VMEM((2, CHUNKS, QUARTER, HALF_CHUNK), f32),
        far_in=pltpu.VMEM((CHUNKS, 2, QUARTER, HALF_CHUNK), f32),
        kept=pltpu.VMEM((CHUNKS, QUARTER, CHUNK), f32),
        load_sem=copies((10,)),
        out_load_sem=copies((CHUNKS,)),
        route_send=copies((len(PIECES),)),
        route_recv=copies((len(PIECES),)),
        near_send=copies((4,)),
        near_recv=copies((4,)),
        far_send=copies((4,)),
        far_recv=copies((4,)),
        pass_send=copies((4,)),
        pass_recv=copies((4,)),
        gather_send=copies((gather_sends,)),
        gather_recv=copies((SEQ, 2)),
        given_sem=copies((2,)),
        near_sum_send=copies((CHUNKS,)),
        near_sum_recv=copies((CHUNKS,)),
        extra_send=copies((CHUNKS,)),
        extra_recv=copies((CHUNKS,)),
        far_sum_send=copies((2, CHUNKS)),
        far_sum_recv=copies((CHUNKS, 2)),
    )


class Refs:
    def __init__(self, **refs):
        self.__dict__.update(refs)


def places():
    me = lax.axis_index("seq")
    head = lax.axis_index("head")
    sibling = head + 1 - 2 * (head % 2)
    return me, head, sibling, (head + 2) % 4, (sibling + 2) % 4


def frame_of(device, place):
    if place < HALF:
        return device * HALF + place
    return (2 * SEQ - 1 - device) * HALF + place - HALF


def angles(r):
    me = lax.axis_index("seq")
    inverse = r.inverse[...]
    for block in range(2):
        first = (me if block == 0 else 2 * SEQ - 1 - me) * BLOCK
        position = first + lax.broadcasted_iota(jnp.int32, (BLOCK, HD), 0)
        angle = position.astype(jnp.float32) * inverse
        rows = pl.ds(block * BLOCK, BLOCK)
        r.cosine[rows, :] = jnp.cos(angle)
        lane = lax.broadcasted_iota(jnp.int32, (BLOCK, HD), 1)
        turned = jnp.sin(angle)
        r.sine[rows, :] = jnp.where(lane < HD // 2, -turned, turned)


def row_of(ref, first, width):
    return ref[pl.ds(first, width)].astype(jnp.float32).reshape(1, width)


def features(r):
    me, head, sibling, pair, cross = places()
    send = [getattr(r, f"send{k}") for k in range(len(PIECES))]
    recv = [getattr(r, f"recv{k}") for k in range(len(PIECES))]
    feat = [getattr(r, f"feat{k}") for k in range(len(PIECES))]

    def pick(device, carry):
        slot = jnp.int32(0)
        for place in range(FR_DEV):
            value = r.source_ref[frame_of(device, place)]
            slot += jnp.where(
                lax.shift_right_logical(value, 4) == me, jnp.bitwise_and(value, 15), 0
            )
        for k, (first, width) in enumerate(PIECES):
            send[k][device] = r.visual[slot, :, pl.ds(first, width)]
        return carry

    lax.fori_loop(0, SEQ, pick, 0)
    pl.semaphore_wait(pltpu.get_barrier_semaphore(), SEQ + 4)

    def route(k, j):
        device = (me + j) % SEQ
        return remote(
            send[k].at[device],
            recv[k].at[me],
            r.route_send.at[k],
            r.route_recv.at[k],
            device,
            route_head(device),
        )

    def routed(k):
        return remote(
            send[k].at[pl.ds(0, SEQ - 1)],
            recv[k].at[pl.ds(0, SEQ - 1)],
            r.route_send.at[k],
            r.route_recv.at[k],
            me,
            sibling,
        )

    for k in range(len(PIECES)):

        def start_route(j, carry):
            route(k, j).start()
            return carry

        lax.fori_loop(1, SEQ, start_route, 0)
        recv[k][me] = send[k][me]
    angles(r)

    def far(label, k):
        block = feat[k].at[label]
        return remote(block, block, r.far_send.at[k], r.far_recv.at[k], me, pair)

    def near_part(label, k):
        block = feat[k].at[label]
        return remote(block, block, r.near_send.at[k], r.near_recv.at[k], me, sibling)

    def passed(label, k):
        block = feat[k].at[label]
        return remote(block, block, r.pass_send.at[k], r.pass_recv.at[k], me, sibling)

    def add_squares(k, label):
        value = feat[k][label].astype(jnp.float32)
        value = value * value
        width = PIECES[k][1]
        total = value[:, :HD]
        for first in range(HD, width, HD):
            total = total + value[:, first : first + HD]
        r.squares[...] += total

    r.squares[...] = jnp.zeros_like(r.squares)
    for k in range(len(PIECES)):
        routed(k).wait_recv()
        for place in range(FR_DEV):
            source = lax.shift_right_logical(r.source_ref[frame_of(me, place)], 4)
            feat[k][head, pl.ds(place * FT, FT), :] = recv[k][source]
        far(head, k).start()
        near_part(head, k).start()
        add_squares(k, head)
        if k > 0:
            far(pair, k - 1).wait_recv()
            passed(pair, k - 1).start()
            near_part(sibling, k - 1).wait_recv()
            add_squares(k - 1, sibling)
            add_squares(k - 1, pair)
        if k > 1:
            passed(cross, k - 2).wait_recv()
            add_squares(k - 2, cross)
    last = len(PIECES) - 1
    near_part(sibling, last).wait_recv()
    add_squares(last, sibling)
    passed(cross, last - 1).wait_recv()
    add_squares(last - 1, cross)
    far(pair, last).wait_recv()
    passed(pair, last).start()
    add_squares(last, pair)
    passed(cross, last).wait_recv()
    add_squares(last, cross)

    def normalize(place, carry):
        rows = pl.ds(pl.multiple_of(place * FT, FT), FT)
        frame = jnp.where(
            place < HALF, me * HALF + place, (2 * SEQ - 1 - me) * HALF + place - HALF
        )
        swapped = lax.shift_right_logical(r.source_ref[frame], 8) != me // 16
        total = jnp.sum(r.squares[rows, :], axis=1, keepdims=True)
        factor = lax.rsqrt(total * (1.0 / MODEL) + 1e-06)
        for k, (first, width) in enumerate(PIECES):
            for part in range(2):
                one = feat[k][part, rows, :]
                two = feat[k][part + 2, rows, :]
                halves = (jnp.where(swapped, two, one), jnp.where(swapped, one, two))
                for i, value in enumerate(halves):
                    column = (part + 2 * i) * PART + first
                    scaled = value.astype(jnp.float32) * factor * row_of(r.gain, column, width)
                    r.normed[rows, pl.ds(column, width)] = scaled.astype(jnp.bfloat16)
        return carry

    lax.fori_loop(0, FR_DEV, normalize, 0)

    def finish():
        for k in range(len(PIECES)):
            routed(k).wait_send()
            far(head, k).wait_send()
            near_part(head, k).wait_send()
            passed(pair, k).wait_send()

    return finish


def route_head(device):
    me, head, _, pair, _ = places()
    return jnp.where(device // 16 == me // 16, head, pair)


def rope(r, value, block):
    rows = pl.ds(block * BLOCK, BLOCK)
    turned = pltpu.roll(value, HD // 2, 1) * r.sine[rows, :]
    return (value * r.cosine[rows, :] + turned).astype(jnp.bfloat16)


def project_keys(r):
    me = lax.axis_index("seq")
    both = jnp.dot(r.normed[...], r.w_kv[...], preferred_element_type=jnp.float32)
    for block in range(2):
        part = both[block * BLOCK : (block + 1) * BLOCK]
        r.buf[me, block, 0] = rope(r, part[:, :HD] + row_of(r.k_bias, 0, HD), block)
        r.buf[me, block, 1] = (part[:, HD:] + row_of(r.v_bias, 0, HD)).astype(jnp.bfloat16)


def project_queries(r):
    for first in range(0, HEADS, 2):
        count = min(2, HEADS - first)
        columns = pl.ds(first * HD, count * HD)
        value = jnp.dot(r.normed[...], r.w_query[:, columns], preferred_element_type=jnp.float32)
        value = value + row_of(r.q_bias, first * HD, count * HD)
        for h in range(count):
            for block in range(2):
                one = value[block * BLOCK : (block + 1) * BLOCK, h * HD : (h + 1) * HD]
                r.q[block, pl.ds((first + h) * BLOCK, BLOCK), :] = rope(r, one, block)


def gather_attend(r):
    me, _, _, y = coordinates()
    head = lax.axis_index("head")
    own = me // 4
    started = []

    def copy_of(source, block, target, send_sem):
        index = near(*source)
        one = r.buf.at[index, block]
        return remote(one, one, send_sem, r.gather_recv.at[index, block], near(*target), head)

    def send(source, block, target):
        started.append(copy_of(source, block, target, r.gather_send.at[len(started)]))
        started[-1].start()

    def attend(kind, dz, dx):
        group = near(dz, dx, 0) // 4
        unit = functools.partial(attend_unit, r.q, r.buf, r.m, r.l, r.acc)
        if (dz, dx) != (0, 0):
            which = jnp.where(group < own, 0, 1)
            if kind == 0:
                unit(1, group, 0, None)
            else:
                unit(which, group, which, None)
            return
        row = lax.broadcasted_iota(jnp.int32, (HEADS, BLOCK, 4 * BLOCK), 1)
        row = row.reshape(HEADS * BLOCK, 4 * BLOCK) + y * BLOCK
        column = lax.broadcasted_iota(jnp.int32, (HEADS * BLOCK, 4 * BLOCK), 1)
        if kind == 0:
            unit(1, group, 0, None)
        elif kind == 1:
            later = column % BLOCK - (column // BLOCK) * BLOCK
            unit(1, group, 1, later <= row - 2 * y * BLOCK)
        else:
            unit(0, group, 0, column <= row)

    for block, target in FIRST_SENDS:
        send((0, 0, 0), block, target)
    project_queries(r)
    plan = gather_plan()
    for code in SCHEDULE:
        if code >= 64:
            attend((code - 64) // 8, (code % 8) // 4, code % 4)
            continue
        block, source = code // 32, ((code // 16) % 2, (code // 4) % 4, code % 4)
        copy_of(source, block, (1, 0, 0), r.gather_send.at[0]).wait_recv()
        for target in plan[(block, *source)]:
            send(source, block, target)

    def finish():
        for copy in started:
            copy.wait_send()

    return finish


def output(r, out):
    me, head, sibling, pair, _ = places()
    other = near(1, 0, 0)
    core = head % 2
    theirs = 2 * ((head // 2 + 1) % 2)
    for which in range(2):
        total = jnp.sum(r.l[which], axis=1, keepdims=True)
        value = (r.acc[which] / total).astype(jnp.bfloat16)
        for h in range(HEADS):
            for half in range(2):
                first = h * BLOCK + half * QUARTER
                r.heads[2 * which + half, :, pl.ds(h * HD, HD)] = value[first : first + QUARTER]
    gift = remote(
        r.heads.at[theirs + 1], r.given, r.given_sem.at[0], r.given_sem.at[1], other, head
    )
    gift.start()
    for place, quarter in enumerate((theirs, sibling, head)):
        r.rows[pl.ds(place * QUARTER, QUARTER), :] = r.heads[quarter]

    def near_copy(j):
        return remote(
            r.near_out.at[j],
            r.near_in.at[j],
            r.near_sum_send.at[j],
            r.near_sum_recv.at[j],
            me,
            sibling,
        )

    def extra_copy(j):
        return remote(
            r.extra_out.at[j],
            r.extra_in.at[j],
            r.extra_send.at[j],
            r.extra_recv.at[j],
            me,
            sibling,
        )

    def far_copy(which, j):
        return remote(
            r.far_out.at[which, j],
            r.far_in.at[j, core],
            r.far_sum_send.at[which, j],
            r.far_sum_recv.at[j, core],
            other if which else me,
            theirs + which,
        )

    def split(value):
        left, right = value[:, :HALF_CHUNK], value[:, HALF_CHUNK:]
        return jnp.where(core == 0, left, right), jnp.where(core == 0, right, left)

    def relay(j):
        near_copy(j).wait_recv()
        r.far_out[0, j] += r.near_in[j, pl.ds(0, QUARTER), :]
        far_copy(0, j).start()
        for half in range(2):
            r.kept[j, :, pl.ds(half * HALF_CHUNK, HALF_CHUNK)] += r.near_in[
                j, pl.ds((half + 1) * QUARTER, QUARTER), :
            ]

    def relay_extra(j):
        extra_copy(j).wait_recv()
        r.far_out[1, j] += r.extra_in[j]
        far_copy(1, j).start()

    for j in range(CHUNKS):
        value = jnp.dot(r.rows[...], r.w_out[j], preferred_element_type=jnp.float32)
        mine, handed = split(value[:QUARTER])
        r.near_out[j, pl.ds(0, QUARTER), :] = handed
        for half in range(2):
            r.near_out[j, pl.ds((half + 1) * QUARTER, QUARTER), :] = value[
                QUARTER : 2 * QUARTER, half * HALF_CHUNK : (half + 1) * HALF_CHUNK
            ]
        near_copy(j).start()
        r.far_out[0, j] = mine
        r.kept[j] = value[2 * QUARTER :]
        if j > 0:
            relay(j - 1)
    relay(CHUNKS - 1)
    gift.wait()
    for j in range(CHUNKS):
        value = jnp.dot(r.given[...], r.w_out[j], preferred_element_type=jnp.float32)
        mine, handed = split(value)
        r.extra_out[j] = handed
        extra_copy(j).start()
        r.far_out[1, j] = mine
        if j > 0:
            relay_extra(j - 1)
    relay_extra(CHUNKS - 1)
    for j in range(CHUNKS):
        for half in range(2):
            remote(
                r.far_out.at[0, j],
                r.far_in.at[j, half],
                r.far_sum_send.at[0, j],
                r.far_sum_recv.at[j, half],
                me,
                pair,
            ).wait_recv()
            columns = pl.ds(half * HALF_CHUNK, HALF_CHUNK)
            total = r.kept[j, :, columns] + r.far_in[j, half]
            out[:, pl.ds(j * CHUNK + half * HALF_CHUNK, HALF_CHUNK)] = total.astype(jnp.bfloat16)
    for j in range(CHUNKS):
        near_copy(j).wait_send()
        extra_copy(j).wait_send()
        for which in range(2):
            far_copy(which, j).wait_send()


INPUTS = (
    "source_hbm",
    "visual_hbm",
    "gain_hbm",
    "q_bias_hbm",
    "k_bias_hbm",
    "v_bias_hbm",
    "inverse_hbm",
    "query_hbm",
    "key_hbm",
    "value_hbm",
    "out_hbm",
)


def kernel(*refs):
    names = INPUTS + ("out",) + tuple(scratch())
    r = Refs(**dict(zip(names, refs)))
    me, head, sibling, pair, cross = places()
    pairs = (
        (r.source_hbm, r.source_ref),
        (r.visual_hbm, r.visual),
        (r.inverse_hbm, r.inverse),
        (r.gain_hbm, r.gain),
        (r.q_bias_hbm, r.q_bias),
        (r.k_bias_hbm, r.k_bias),
        (r.v_bias_hbm, r.v_bias),
        (r.key_hbm, r.w_kv.at[:, pl.ds(0, HD)]),
        (r.value_hbm, r.w_kv.at[:, pl.ds(HD, HD)]),
        (r.query_hbm, r.w_query),
    )
    loads = [pltpu.make_async_copy(a, b, r.load_sem.at[i]) for i, (a, b) in enumerate(pairs)]
    for j in range(CHUNKS):
        block = r.out_hbm.at[:, pl.ds(j * CHUNK, CHUNK)]
        loads.append(pltpu.make_async_copy(block, r.w_out.at[j], r.out_load_sem.at[j]))
    for load in loads[:2]:
        load.start()
    def greet_seq(j, carry):
        device = (me + j) % SEQ
        greet(barrier, device, route_head(device))
        return carry

    barrier = pltpu.get_barrier_semaphore()
    lax.fori_loop(1, SEQ, greet_seq, 0)
    for each in (sibling, pair, cross):
        greet(barrier, me, each)
    for each in (head, cross):
        greet(barrier, near(1, 0, 0), each)
    for load in loads[2:]:
        load.start()
    r.m[...] = jnp.full_like(r.m, NEG)
    r.l[...] = jnp.zeros_like(r.l)
    r.acc[...] = jnp.zeros_like(r.acc)
    for load in loads[:7]:
        load.wait()
    endings = [features(r)]
    for load in loads[7:]:
        load.wait()
    project_keys(r)
    endings.append(gather_attend(r))
    output(r, r.out)
    for ending in endings:
        ending()


def on_device(
    visual, frame_source, input_norm_gain, w_query, w_key, w_value, q_bias, k_bias, v_bias, w_out
):
    inverse = 1000000.0 ** (-(np.arange(HD // 2) * 2.0) / HD)
    inverse = jnp.asarray(np.concatenate([inverse, inverse])[None], jnp.float32)
    return pl.pallas_call(
        kernel,
        out_shape=jax.ShapeDtypeStruct((QUARTER, MODEL), jnp.bfloat16),
        in_specs=[ANY] * len(INPUTS),
        out_specs=VMEM,
        scratch_shapes=list(scratch().values()),
        compiler_params=pltpu.CompilerParams(
            collective_id=1, has_side_effects=True, vmem_limit_bytes=62 << 20
        ),
    )(
        frame_source,
        visual.reshape(FR_DEV, FT, PART),
        input_norm_gain,
        q_bias,
        k_bias,
        v_bias,
        inverse,
        w_query,
        w_key,
        w_value,
        w_out,
    )


def solution(mesh):
    placed = (
        P("seq", "head"),
        P(),
        P(),
        P(None, "head"),
        P(None, "head"),
        P(None, "head"),
        P("head"),
        P("head"),
        P("head"),
        P("head", None),
    )
    return jax.shard_map(
        on_device, mesh=mesh, in_specs=placed, out_specs=P(("seq", "head"), None), check_vma=False
    )
```

```python
import functools
import math

import jax
import jax.numpy as jnp
import numpy as np
from jax import lax
from jax.experimental import pallas as pl
from jax.experimental.pallas import tpu as pltpu
from jax.sharding import PartitionSpec as P

HD = 128
HEADS = 7
FT = 16
FR_DEV = 16
HALF = FR_DEV // 2
SEQ = 32
TOK_DEV = 256
BLOCK = 128
QUARTER = 64
MODEL = 3584
PART = MODEL // 4
MESH = pl.DeviceIdType.MESH
NEG = -1e30
EXP_SCALE = math.log2(math.e) / math.sqrt(HD)
VMEM = pl.BlockSpec(memory_space=pltpu.VMEM)
ANY = pl.BlockSpec(memory_space=pl.ANY)
CHUNK = 512
CHUNKS = MODEL // CHUNK


def remote(src, dst, send_sem, recv_sem, seq, head):
    return pltpu.make_async_remote_copy(
        src_ref=src,
        dst_ref=dst,
        send_sem=send_sem,
        recv_sem=recv_sem,
        device_id=(seq, head),
        device_id_type=MESH,
    )

HALF_CHUNK = CHUNK // 2
DIRECT = 16
GIVEN = QUARTER - DIRECT
PIECES = ((0, 512), (512, 384))

SCHEDULE = (
    33, 4, 35, 1, 3, 12, 44, 34, 7, 16, 72, 47, 45, 37, 49, 2,
    48, 8, 36, 5, 80, 15, 20, 13, 64, 38, 28, 6, 39, 51, 65, 43,
    9, 50, 53, 19, 40, 46, 17, 73, 21, 18, 68, 76, 24, 14, 52, 11,
    67, 75, 54, 55, 41, 10, 66, 22, 63, 61, 31, 23, 25, 42, 29, 69,
    77, 27, 57, 60, 74, 26, 70, 30, 62, 59, 71, 58, 56, 79, 78,
)
BY_Z = ((1, 0, 2), (1, 2, 1), (1, 2, 2))
PLUS = ((0, 2), (1, 1))
FIRST_FAR = (1, 1)


def coordinates():
    me = lax.axis_index("seq")
    return me, me // 16, (me // 4) % 4, me % 4


def near(dz, dx, dy):
    _, z, x, y = coordinates()
    return ((z + dz) % 2) * 16 + ((x + dx) % 4) * 4 + (y + dy) % 4


def comes_from(block, source):
    dz, dx, dy = source
    first, last = (dx, dy) if block == 0 else (dy, dx)
    if last == 0:
        if dz:
            return (1, 0, 0)
        step, along_x = first if first != 2 else FIRST_FAR[block], block == 0
    elif (dz, first, last) in BY_Z:
        return (1, 0, 0)
    elif last != 2:
        step, along_x = last, block == 1
    else:
        step, along_x = 1 if (dz, first) in PLUS else 3, block == 1
    return (0, step, 0) if along_x else (0, 0, step)


def gather_plan():
    plan = {}
    for block in range(2):
        for code in range(32):
            source = (code // 16, (code // 4) % 4, code % 4)
            targets = []
            for step in ((1, 0, 0), (0, 1, 0), (0, 3, 0), (0, 0, 1), (0, 0, 3)):
                back = ((2 - step[0]) % 2, (4 - step[1]) % 4, (4 - step[2]) % 4)
                seen = (
                    (source[0] - step[0]) % 2,
                    (source[1] - step[1]) % 4,
                    (source[2] - step[2]) % 4,
                )
                if seen != (0, 0, 0) and comes_from(block, seen) == back:
                    targets.append(step)
            plan[(block, *source)] = targets
    return plan


def attend_unit(q, buf, m, l, acc, which, group, block, keep):
    keys = buf[pl.ds(group * 4, 4), block, 0].reshape(4 * BLOCK, HD)
    vals = buf[pl.ds(group * 4, 4), block, 1].reshape(4 * BLOCK, HD)
    s = lax.dot_general(
        q[which], keys, (((1,), (1,)), ((), ())), preferred_element_type=jnp.float32
    )
    if keep is not None:
        s = jnp.where(keep, s, NEG)
    old = m[which]
    new = jnp.maximum(old, jnp.max(s, axis=1, keepdims=True))
    fade = jnp.exp2((old - new) * EXP_SCALE)
    p = jnp.exp2((s - jnp.concatenate([new] * 4, axis=1)) * EXP_SCALE)
    parts = p[:, :128] + p[:, 128:256] + p[:, 256:384] + p[:, 384:]
    l[which] = l[which] * fade + parts
    acc[which] = acc[which] * fade + jnp.dot(
        p.astype(jnp.bfloat16), vals, preferred_element_type=jnp.float32
    )
    m[which] = new


FIRST_SENDS = (
    (1, (0, 0, 3)),
    (0, (0, 3, 0)),
    (0, (1, 0, 0)),
    (1, (1, 0, 0)),
    (1, (0, 1, 0)),
    (0, (0, 0, 3)),
    (1, (0, 0, 1)),
    (0, (0, 0, 1)),
    (0, (0, 1, 0)),
    (1, (0, 3, 0)),
)


def greet(barrier, seq, head):
    pl.semaphore_signal(barrier, inc=1, device_id=(seq, head), device_id_type=MESH)


def scratch():
    copies = pltpu.SemaphoreType.DMA
    bf16 = jnp.bfloat16
    f32 = jnp.float32
    gather_sends = sum(len(targets) for targets in gather_plan().values())
    state = pltpu.VMEM((2, HEADS * BLOCK, HD), f32)
    return dict(
        source_ref=pltpu.SMEM((SEQ * FR_DEV,), jnp.int32),
        visual=pltpu.VMEM((FR_DEV, FT, PART), bf16),
        gain=pltpu.VMEM((MODEL,), bf16),
        q_bias=pltpu.VMEM((PART,), bf16),
        k_bias=pltpu.VMEM((HD,), bf16),
        v_bias=pltpu.VMEM((HD,), bf16),
        inverse=pltpu.VMEM((1, HD), f32),
        **{f"send{k}": pltpu.VMEM((SEQ, FT, w), bf16) for k, (_, w) in enumerate(PIECES)},
        **{f"recv{k}": pltpu.VMEM((SEQ, FT, w), bf16) for k, (_, w) in enumerate(PIECES)},
        **{f"feat{k}": pltpu.VMEM((4, TOK_DEV, w), bf16) for k, (_, w) in enumerate(PIECES)},
        squares=pltpu.VMEM((TOK_DEV, HD), f32),
        normed=pltpu.VMEM((TOK_DEV, MODEL), bf16),
        w_query=pltpu.VMEM((MODEL, PART), bf16),
        w_kv=pltpu.VMEM((MODEL, 2 * HD), bf16),
        w_out=pltpu.VMEM((CHUNKS, PART, CHUNK), bf16),
        cosine=pltpu.VMEM((TOK_DEV, HD), f32),
        sine=pltpu.VMEM((TOK_DEV, HD), f32),
        q=pltpu.VMEM((2, HEADS * BLOCK, HD), bf16),
        buf=pltpu.VMEM((SEQ, 2, 2, BLOCK, HD), bf16),
        m=state,
        l=state,
        acc=state,
        heads=pltpu.VMEM((4, QUARTER, PART), bf16),
        rows=pltpu.VMEM((3 * QUARTER + DIRECT, PART), bf16),
        given=pltpu.VMEM((GIVEN, PART), bf16),
        near_out=pltpu.VMEM((CHUNKS, 3 * QUARTER + DIRECT, HALF_CHUNK), f32),
        near_in=pltpu.VMEM((CHUNKS, 3 * QUARTER + DIRECT, HALF_CHUNK), f32),
        extra_out=pltpu.VMEM((CHUNKS, GIVEN, HALF_CHUNK), f32),
        extra_in=pltpu.VMEM((CHUNKS, GIVEN, HALF_CHUNK), f32),
        far_out=pltpu.VMEM((2, CHUNKS, QUARTER, HALF_CHUNK), f32),
        far_in=pltpu.VMEM((CHUNKS, 2, QUARTER, HALF_CHUNK), f32),
        kept=pltpu.VMEM((CHUNKS, QUARTER, CHUNK), f32),
        load_sem=copies((10,)),
        out_load_sem=copies((CHUNKS,)),
        route_send=copies((len(PIECES),)),
        route_recv=copies((len(PIECES),)),
        near_send=copies((4,)),
        near_recv=copies((4,)),
        far_send=copies((4,)),
        far_recv=copies((4,)),
        pass_send=copies((4,)),
        pass_recv=copies((4,)),
        gather_send=copies((gather_sends,)),
        gather_recv=copies((SEQ, 2)),
        given_sem=copies((2,)),
        near_sum_send=copies((CHUNKS,)),
        near_sum_recv=copies((CHUNKS,)),
        extra_send=copies((CHUNKS,)),
        extra_recv=copies((CHUNKS,)),
        far_sum_send=copies((2, CHUNKS, 2)),
        far_sum_recv=copies((CHUNKS, 2, 2)),
    )


class Refs:
    def __init__(self, **refs):
        self.__dict__.update(refs)


def places():
    me = lax.axis_index("seq")
    head = lax.axis_index("head")
    sibling = head + 1 - 2 * (head % 2)
    return me, head, sibling, (head + 2) % 4, (sibling + 2) % 4


def frame_of(device, place):
    if place < HALF:
        return device * HALF + place
    return (2 * SEQ - 1 - device) * HALF + place - HALF


def angles(r):
    me = lax.axis_index("seq")
    inverse = r.inverse[...]
    for block in range(2):
        first = (me if block == 0 else 2 * SEQ - 1 - me) * BLOCK
        position = first + lax.broadcasted_iota(jnp.int32, (BLOCK, HD), 0)
        angle = position.astype(jnp.float32) * inverse
        rows = pl.ds(block * BLOCK, BLOCK)
        r.cosine[rows, :] = jnp.cos(angle)
        lane = lax.broadcasted_iota(jnp.int32, (BLOCK, HD), 1)
        turned = jnp.sin(angle)
        r.sine[rows, :] = jnp.where(lane < HD // 2, -turned, turned)


def row_of(ref, first, width):
    return ref[pl.ds(first, width)].astype(jnp.float32).reshape(1, width)


def features(r):
    me, head, sibling, pair, cross = places()
    send = [getattr(r, f"send{k}") for k in range(len(PIECES))]
    recv = [getattr(r, f"recv{k}") for k in range(len(PIECES))]
    feat = [getattr(r, f"feat{k}") for k in range(len(PIECES))]

    def pick(device, carry):
        slot = jnp.int32(0)
        for place in range(FR_DEV):
            value = r.source_ref[frame_of(device, place)]
            slot += jnp.where(
                lax.shift_right_logical(value, 4) == me, jnp.bitwise_and(value, 15), 0
            )
        for k, (first, width) in enumerate(PIECES):
            send[k][device] = r.visual[slot, :, pl.ds(first, width)]
        return carry

    lax.fori_loop(0, SEQ, pick, 0)
    pl.semaphore_wait(pltpu.get_barrier_semaphore(), SEQ + 4)

    def route(k, j):
        device = (me + j) % SEQ
        return remote(
            send[k].at[device],
            recv[k].at[me],
            r.route_send.at[k],
            r.route_recv.at[k],
            device,
            route_head(device),
        )

    def routed(k):
        return remote(
            send[k].at[pl.ds(0, SEQ - 1)],
            recv[k].at[pl.ds(0, SEQ - 1)],
            r.route_send.at[k],
            r.route_recv.at[k],
            me,
            sibling,
        )

    for k in range(len(PIECES)):

        def start_route(j, carry):
            route(k, j).start()
            return carry

        lax.fori_loop(1, SEQ, start_route, 0)
        recv[k][me] = send[k][me]
    angles(r)

    def far(label, k):
        block = feat[k].at[label]
        return remote(block, block, r.far_send.at[k], r.far_recv.at[k], me, pair)

    def near_part(label, k):
        block = feat[k].at[label]
        return remote(block, block, r.near_send.at[k], r.near_recv.at[k], me, sibling)

    def passed(label, k):
        block = feat[k].at[label]
        return remote(block, block, r.pass_send.at[k], r.pass_recv.at[k], me, sibling)

    def add_squares(k, label):
        value = feat[k][label].astype(jnp.float32)
        value = value * value
        width = PIECES[k][1]
        total = value[:, :HD]
        for first in range(HD, width, HD):
            total = total + value[:, first : first + HD]
        r.squares[...] += total

    r.squares[...] = jnp.zeros_like(r.squares)
    for k in range(len(PIECES)):
        routed(k).wait_recv()
        for place in range(FR_DEV):
            source = lax.shift_right_logical(r.source_ref[frame_of(me, place)], 4)
            feat[k][head, pl.ds(place * FT, FT), :] = recv[k][source]
        far(head, k).start()
        near_part(head, k).start()
        add_squares(k, head)
        if k > 0:
            far(pair, k - 1).wait_recv()
            passed(pair, k - 1).start()
            near_part(sibling, k - 1).wait_recv()
            add_squares(k - 1, sibling)
            add_squares(k - 1, pair)
        if k > 1:
            passed(cross, k - 2).wait_recv()
            add_squares(k - 2, cross)
    last = len(PIECES) - 1
    near_part(sibling, last).wait_recv()
    add_squares(last, sibling)
    passed(cross, last - 1).wait_recv()
    add_squares(last - 1, cross)
    far(pair, last).wait_recv()
    passed(pair, last).start()
    add_squares(last, pair)
    passed(cross, last).wait_recv()
    add_squares(last, cross)

    def normalize(place, carry):
        rows = pl.ds(pl.multiple_of(place * FT, FT), FT)
        frame = jnp.where(
            place < HALF, me * HALF + place, (2 * SEQ - 1 - me) * HALF + place - HALF
        )
        swapped = lax.shift_right_logical(r.source_ref[frame], 8) != me // 16
        total = jnp.sum(r.squares[rows, :], axis=1, keepdims=True)
        factor = lax.rsqrt(total * (1.0 / MODEL) + 1e-06)
        for k, (first, width) in enumerate(PIECES):
            for part in range(2):
                one = feat[k][part, rows, :]
                two = feat[k][part + 2, rows, :]
                halves = (jnp.where(swapped, two, one), jnp.where(swapped, one, two))
                for i, value in enumerate(halves):
                    column = (part + 2 * i) * PART + first
                    scaled = value.astype(jnp.float32) * factor * row_of(r.gain, column, width)
                    r.normed[rows, pl.ds(column, width)] = scaled.astype(jnp.bfloat16)
        return carry

    lax.fori_loop(0, FR_DEV, normalize, 0)

    def finish():
        for k in range(len(PIECES)):
            routed(k).wait_send()
            far(head, k).wait_send()
            near_part(head, k).wait_send()
            passed(pair, k).wait_send()

    return finish


def route_head(device):
    me, head, _, pair, _ = places()
    return jnp.where(device // 16 == me // 16, head, pair)


def rope(r, value, block):
    rows = pl.ds(block * BLOCK, BLOCK)
    turned = pltpu.roll(value, HD // 2, 1) * r.sine[rows, :]
    return (value * r.cosine[rows, :] + turned).astype(jnp.bfloat16)


def project_keys(r):
    me = lax.axis_index("seq")
    both = jnp.dot(r.normed[...], r.w_kv[...], preferred_element_type=jnp.float32)
    for block in range(2):
        part = both[block * BLOCK : (block + 1) * BLOCK]
        r.buf[me, block, 0] = rope(r, part[:, :HD] + row_of(r.k_bias, 0, HD), block)
        r.buf[me, block, 1] = (part[:, HD:] + row_of(r.v_bias, 0, HD)).astype(jnp.bfloat16)


def project_queries(r):
    for first in range(0, HEADS, 2):
        count = min(2, HEADS - first)
        columns = pl.ds(first * HD, count * HD)
        value = jnp.dot(r.normed[...], r.w_query[:, columns], preferred_element_type=jnp.float32)
        value = value + row_of(r.q_bias, first * HD, count * HD)
        for h in range(count):
            for block in range(2):
                one = value[block * BLOCK : (block + 1) * BLOCK, h * HD : (h + 1) * HD]
                r.q[block, pl.ds((first + h) * BLOCK, BLOCK), :] = rope(r, one, block)


def gather_attend(r):
    me, _, _, y = coordinates()
    head = lax.axis_index("head")
    own = me // 4
    started = []

    def copy_of(source, block, target, send_sem):
        index = near(*source)
        one = r.buf.at[index, block]
        return remote(one, one, send_sem, r.gather_recv.at[index, block], near(*target), head)

    def send(source, block, target):
        started.append(copy_of(source, block, target, r.gather_send.at[len(started)]))
        started[-1].start()

    def attend(kind, dz, dx):
        group = near(dz, dx, 0) // 4
        unit = functools.partial(attend_unit, r.q, r.buf, r.m, r.l, r.acc)
        if (dz, dx) != (0, 0):
            which = jnp.where(group < own, 0, 1)
            if kind == 0:
                unit(1, group, 0, None)
            else:
                unit(which, group, which, None)
            return
        row = lax.broadcasted_iota(jnp.int32, (HEADS, BLOCK, 4 * BLOCK), 1)
        row = row.reshape(HEADS * BLOCK, 4 * BLOCK) + y * BLOCK
        column = lax.broadcasted_iota(jnp.int32, (HEADS * BLOCK, 4 * BLOCK), 1)
        if kind == 0:
            unit(1, group, 0, None)
        elif kind == 1:
            later = column % BLOCK - (column // BLOCK) * BLOCK
            unit(1, group, 1, later <= row - 2 * y * BLOCK)
        else:
            unit(0, group, 0, column <= row)

    for block, target in FIRST_SENDS:
        send((0, 0, 0), block, target)
    project_queries(r)
    plan = gather_plan()
    for code in SCHEDULE:
        if code >= 64:
            attend((code - 64) // 8, (code % 8) // 4, code % 4)
            continue
        block, source = code // 32, ((code // 16) % 2, (code // 4) % 4, code % 4)
        copy_of(source, block, (1, 0, 0), r.gather_send.at[0]).wait_recv()
        for target in plan[(block, *source)]:
            send(source, block, target)

    def finish():
        for copy in started:
            copy.wait_send()

    return finish


def output(r, out):
    me, head, sibling, pair, _ = places()
    other = near(1, 0, 0)
    core = head % 2
    theirs = 2 * ((head // 2 + 1) % 2)
    for which in range(2):
        total = jnp.sum(r.l[which], axis=1, keepdims=True)
        value = (r.acc[which] / total).astype(jnp.bfloat16)
        for h in range(HEADS):
            for half in range(2):
                first = h * BLOCK + half * QUARTER
                r.heads[2 * which + half, :, pl.ds(h * HD, HD)] = value[first : first + QUARTER]
    gift = remote(
        r.heads.at[theirs + 1, pl.ds(DIRECT, GIVEN), :],
        r.given,
        r.given_sem.at[0],
        r.given_sem.at[1],
        other,
        head,
    )
    gift.start()
    for place, quarter in enumerate((theirs, sibling, head)):
        r.rows[pl.ds(place * QUARTER, QUARTER), :] = r.heads[quarter]
    r.rows[pl.ds(3 * QUARTER, DIRECT), :] = r.heads[theirs + 1, pl.ds(0, DIRECT), :]

    def near_copy(j):
        return remote(
            r.near_out.at[j],
            r.near_in.at[j],
            r.near_sum_send.at[j],
            r.near_sum_recv.at[j],
            me,
            sibling,
        )

    def extra_copy(j):
        return remote(
            r.extra_out.at[j],
            r.extra_in.at[j],
            r.extra_send.at[j],
            r.extra_recv.at[j],
            me,
            sibling,
        )

    parts = (pl.ds(0, DIRECT), pl.ds(DIRECT, GIVEN))

    def far_copy(which, j, part):
        return remote(
            r.far_out.at[which, j, parts[part], :],
            r.far_in.at[j, core, parts[part], :],
            r.far_sum_send.at[which, j, part],
            r.far_sum_recv.at[j, core, part],
            other if which and part else me,
            theirs + which,
        )

    def split(value):
        left, right = value[:, :HALF_CHUNK], value[:, HALF_CHUNK:]
        return jnp.where(core == 0, left, right), jnp.where(core == 0, right, left)

    def relay(j):
        near_copy(j).wait_recv()
        r.far_out[0, j] += r.near_in[j, pl.ds(0, QUARTER), :]
        for part in range(2):
            far_copy(0, j, part).start()
        r.far_out[1, j, parts[0], :] += r.near_in[j, pl.ds(3 * QUARTER, DIRECT), :]
        far_copy(1, j, 0).start()
        for half in range(2):
            r.kept[j, :, pl.ds(half * HALF_CHUNK, HALF_CHUNK)] += r.near_in[
                j, pl.ds((half + 1) * QUARTER, QUARTER), :
            ]

    def relay_extra(j):
        extra_copy(j).wait_recv()
        r.far_out[1, j, parts[1], :] += r.extra_in[j]
        far_copy(1, j, 1).start()

    for j in range(CHUNKS):
        value = jnp.dot(r.rows[...], r.w_out[j], preferred_element_type=jnp.float32)
        mine, handed = split(value[:QUARTER])
        r.near_out[j, pl.ds(0, QUARTER), :] = handed
        for half in range(2):
            r.near_out[j, pl.ds((half + 1) * QUARTER, QUARTER), :] = value[
                QUARTER : 2 * QUARTER, half * HALF_CHUNK : (half + 1) * HALF_CHUNK
            ]
        r.far_out[0, j] = mine
        mine, handed = split(value[3 * QUARTER :])
        r.near_out[j, pl.ds(3 * QUARTER, DIRECT), :] = handed
        near_copy(j).start()
        r.far_out[1, j, parts[0], :] = mine
        r.kept[j] = value[2 * QUARTER : 3 * QUARTER]
        if j > 0:
            relay(j - 1)
    relay(CHUNKS - 1)
    gift.wait()
    for j in range(CHUNKS):
        value = jnp.dot(r.given[...], r.w_out[j], preferred_element_type=jnp.float32)
        mine, handed = split(value)
        r.extra_out[j] = handed
        extra_copy(j).start()
        r.far_out[1, j, parts[1], :] = mine
        if j > 0:
            relay_extra(j - 1)
    relay_extra(CHUNKS - 1)
    for j in range(CHUNKS):
        for half in range(2):
            for part in range(2):
                remote(
                    r.far_out.at[0, j, parts[part], :],
                    r.far_in.at[j, half, parts[part], :],
                    r.far_sum_send.at[0, j, part],
                    r.far_sum_recv.at[j, half, part],
                    me,
                    pair,
                ).wait_recv()
            columns = pl.ds(half * HALF_CHUNK, HALF_CHUNK)
            total = r.kept[j, :, columns] + r.far_in[j, half]
            out[:, pl.ds(j * CHUNK + half * HALF_CHUNK, HALF_CHUNK)] = total.astype(jnp.bfloat16)
    for j in range(CHUNKS):
        near_copy(j).wait_send()
        extra_copy(j).wait_send()
        for which in range(2):
            for part in range(2):
                far_copy(which, j, part).wait_send()


INPUTS = (
    "source_hbm",
    "visual_hbm",
    "gain_hbm",
    "q_bias_hbm",
    "k_bias_hbm",
    "v_bias_hbm",
    "inverse_hbm",
    "query_hbm",
    "key_hbm",
    "value_hbm",
    "out_hbm",
)


def kernel(*refs):
    names = INPUTS + ("out",) + tuple(scratch())
    r = Refs(**dict(zip(names, refs)))
    me, head, sibling, pair, cross = places()
    pairs = (
        (r.source_hbm, r.source_ref),
        (r.visual_hbm, r.visual),
        (r.inverse_hbm, r.inverse),
        (r.gain_hbm, r.gain),
        (r.q_bias_hbm, r.q_bias),
        (r.k_bias_hbm, r.k_bias),
        (r.v_bias_hbm, r.v_bias),
        (r.key_hbm, r.w_kv.at[:, pl.ds(0, HD)]),
        (r.value_hbm, r.w_kv.at[:, pl.ds(HD, HD)]),
        (r.query_hbm, r.w_query),
    )
    loads = [pltpu.make_async_copy(a, b, r.load_sem.at[i]) for i, (a, b) in enumerate(pairs)]
    for j in range(CHUNKS):
        block = r.out_hbm.at[:, pl.ds(j * CHUNK, CHUNK)]
        loads.append(pltpu.make_async_copy(block, r.w_out.at[j], r.out_load_sem.at[j]))
    for load in loads[:2]:
        load.start()
    def greet_seq(j, carry):
        device = (me + j) % SEQ
        greet(barrier, device, route_head(device))
        return carry

    barrier = pltpu.get_barrier_semaphore()
    lax.fori_loop(1, SEQ, greet_seq, 0)
    for each in (sibling, pair, cross):
        greet(barrier, me, each)
    for each in (head, cross):
        greet(barrier, near(1, 0, 0), each)
    for load in loads[2:]:
        load.start()
    r.m[...] = jnp.full_like(r.m, NEG)
    r.l[...] = jnp.zeros_like(r.l)
    r.acc[...] = jnp.zeros_like(r.acc)
    for load in loads[:7]:
        load.wait()
    endings = [features(r)]
    for load in loads[7:]:
        load.wait()
    project_keys(r)
    endings.append(gather_attend(r))
    output(r, r.out)
    for ending in endings:
        ending()


def on_device(
    visual, frame_source, input_norm_gain, w_query, w_key, w_value, q_bias, k_bias, v_bias, w_out
):
    inverse = 1000000.0 ** (-(np.arange(HD // 2) * 2.0) / HD)
    inverse = jnp.asarray(np.concatenate([inverse, inverse])[None], jnp.float32)
    return pl.pallas_call(
        kernel,
        out_shape=jax.ShapeDtypeStruct((QUARTER, MODEL), jnp.bfloat16),
        in_specs=[ANY] * len(INPUTS),
        out_specs=VMEM,
        scratch_shapes=list(scratch().values()),
        compiler_params=pltpu.CompilerParams(
            collective_id=1, has_side_effects=True, vmem_limit_bytes=62 << 20
        ),
    )(
        frame_source,
        visual.reshape(FR_DEV, FT, PART),
        input_norm_gain,
        q_bias,
        k_bias,
        v_bias,
        inverse,
        w_query,
        w_key,
        w_value,
        w_out,
    )


def solution(mesh):
    placed = (
        P("seq", "head"),
        P(),
        P(),
        P(None, "head"),
        P(None, "head"),
        P(None, "head"),
        P("head"),
        P("head"),
        P("head"),
        P("head", None),
    )
    return jax.shard_map(
        on_device, mesh=mesh, in_specs=placed, out_specs=P(("seq", "head"), None), check_vma=False
    )
```

```python
import functools
import math

import jax
import jax.numpy as jnp
import numpy as np
from jax import lax
from jax.experimental import pallas as pl
from jax.experimental.pallas import tpu as pltpu
from jax.sharding import PartitionSpec as P

HD = 128
HEADS = 7
FT = 16
FR_DEV = 16
HALF = FR_DEV // 2
SEQ = 32
TOK_DEV = 256
BLOCK = 128
QUARTER = 64
MODEL = 3584
PART = MODEL // 4
MESH = pl.DeviceIdType.MESH
NEG = -1e30
EXP_SCALE = math.log2(math.e) / math.sqrt(HD)
VMEM = pl.BlockSpec(memory_space=pltpu.VMEM)
ANY = pl.BlockSpec(memory_space=pl.ANY)
CHUNK = 512
CHUNKS = MODEL // CHUNK


def remote(src, dst, send_sem, recv_sem, seq, head):
    return pltpu.make_async_remote_copy(
        src_ref=src,
        dst_ref=dst,
        send_sem=send_sem,
        recv_sem=recv_sem,
        device_id=(seq, head),
        device_id_type=MESH,
    )

HALF_CHUNK = CHUNK // 2
DIRECT = 16
GIVEN = QUARTER - DIRECT
PIECES = ((0, 512), (512, 384))

SCHEDULE = (
    3, 4, 35, 16, 33, 12, 2, 5, 44, 1, 48, 80, 47, 34, 8, 64,
    19, 7, 39, 51, 37, 49, 72, 15, 40, 6, 28, 45, 13, 65, 38, 36,
    9, 73, 43, 17, 20, 18, 11, 55, 68, 41, 50, 46, 29, 76, 24, 14,
    60, 67, 31, 10, 75, 42, 66, 74, 62, 53, 27, 23, 63, 22, 54, 61,
    52, 30, 71, 79, 25, 21, 56, 69, 77, 26, 58, 57, 59, 70, 78,
)
BY_Z = ((1, 0, 1), (1, 1, 2), (1, 2, 1))
PLUS = ((0, 1), (0, 2), (1, 3))
FIRST_FAR = (1, 1)


def coordinates():
    me = lax.axis_index("seq")
    return me, me // 16, (me // 4) % 4, me % 4


def near(dz, dx, dy):
    _, z, x, y = coordinates()
    return ((z + dz) % 2) * 16 + ((x + dx) % 4) * 4 + (y + dy) % 4


def comes_from(block, source):
    dz, dx, dy = source
    first, last = (dx, dy) if block == 0 else (dy, dx)
    if last == 0:
        if dz:
            return (1, 0, 0)
        step, along_x = first if first != 2 else FIRST_FAR[block], block == 0
    elif (dz, first, last) in BY_Z:
        return (1, 0, 0)
    elif last != 2:
        step, along_x = last, block == 1
    else:
        step, along_x = 1 if (dz, first) in PLUS else 3, block == 1
    return (0, step, 0) if along_x else (0, 0, step)


def gather_plan():
    plan = {}
    for block in range(2):
        for code in range(32):
            source = (code // 16, (code // 4) % 4, code % 4)
            targets = []
            for step in ((1, 0, 0), (0, 1, 0), (0, 3, 0), (0, 0, 1), (0, 0, 3)):
                back = ((2 - step[0]) % 2, (4 - step[1]) % 4, (4 - step[2]) % 4)
                seen = (
                    (source[0] - step[0]) % 2,
                    (source[1] - step[1]) % 4,
                    (source[2] - step[2]) % 4,
                )
                if seen != (0, 0, 0) and comes_from(block, seen) == back:
                    targets.append(step)
            plan[(block, *source)] = targets
    return plan


def attend_unit(q, buf, m, l, acc, which, group, block, keep):
    keys = buf[pl.ds(group * 4, 4), block, 0].reshape(4 * BLOCK, HD)
    vals = buf[pl.ds(group * 4, 4), block, 1].reshape(4 * BLOCK, HD)
    s = lax.dot_general(
        q[which], keys, (((1,), (1,)), ((), ())), preferred_element_type=jnp.float32
    )
    if keep is not None:
        s = jnp.where(keep, s, NEG)
    old = m[which]
    new = jnp.maximum(old, jnp.max(s, axis=1, keepdims=True))
    fade = jnp.exp2((old - new) * EXP_SCALE)
    p = jnp.exp2((s - jnp.concatenate([new] * 4, axis=1)) * EXP_SCALE)
    parts = p[:, :128] + p[:, 128:256] + p[:, 256:384] + p[:, 384:]
    l[which] = l[which] * fade + parts
    acc[which] = acc[which] * fade + jnp.dot(
        p.astype(jnp.bfloat16), vals, preferred_element_type=jnp.float32
    )
    m[which] = new


FIRST_SENDS = (
    (0, (1, 0, 0)),
    (1, (0, 0, 1)),
    (1, (0, 3, 0)),
    (1, (0, 1, 0)),
    (0, (0, 3, 0)),
    (0, (0, 0, 3)),
    (1, (0, 0, 3)),
    (0, (0, 1, 0)),
    (0, (0, 0, 1)),
    (1, (1, 0, 0)),
)


def greet(barrier, seq, head):
    pl.semaphore_signal(barrier, inc=1, device_id=(seq, head), device_id_type=MESH)


def scratch():
    copies = pltpu.SemaphoreType.DMA
    bf16 = jnp.bfloat16
    f32 = jnp.float32
    gather_sends = sum(len(targets) for targets in gather_plan().values())
    state = pltpu.VMEM((2, HEADS * BLOCK, HD), f32)
    return dict(
        source_ref=pltpu.SMEM((SEQ * FR_DEV,), jnp.int32),
        visual=pltpu.VMEM((FR_DEV, FT, PART), bf16),
        gain=pltpu.VMEM((MODEL,), bf16),
        q_bias=pltpu.VMEM((PART,), bf16),
        k_bias=pltpu.VMEM((HD,), bf16),
        v_bias=pltpu.VMEM((HD,), bf16),
        inverse=pltpu.VMEM((1, HD), f32),
        **{f"send{k}": pltpu.VMEM((SEQ, FT, w), bf16) for k, (_, w) in enumerate(PIECES)},
        **{f"recv{k}": pltpu.VMEM((SEQ, FT, w), bf16) for k, (_, w) in enumerate(PIECES)},
        **{f"feat{k}": pltpu.VMEM((4, TOK_DEV, w), bf16) for k, (_, w) in enumerate(PIECES)},
        squares=pltpu.VMEM((TOK_DEV, HD), f32),
        normed=pltpu.VMEM((TOK_DEV, MODEL), bf16),
        w_query=pltpu.VMEM((MODEL, PART), bf16),
        w_kv=pltpu.VMEM((MODEL, 2 * HD), bf16),
        w_out=pltpu.VMEM((CHUNKS, PART, CHUNK), bf16),
        cosine=pltpu.VMEM((TOK_DEV, HD), f32),
        sine=pltpu.VMEM((TOK_DEV, HD), f32),
        q=pltpu.VMEM((2, HEADS * BLOCK, HD), bf16),
        buf=pltpu.VMEM((SEQ, 2, 2, BLOCK, HD), bf16),
        m=state,
        l=state,
        acc=state,
        heads=pltpu.VMEM((4, QUARTER, PART), bf16),
        rows=pltpu.VMEM((3 * QUARTER + DIRECT, PART), bf16),
        given=pltpu.VMEM((GIVEN, PART), bf16),
        near_out=pltpu.VMEM((CHUNKS, 3 * QUARTER + DIRECT, HALF_CHUNK), f32),
        near_in=pltpu.VMEM((CHUNKS, 3 * QUARTER + DIRECT, HALF_CHUNK), f32),
        extra_out=pltpu.VMEM((CHUNKS, GIVEN, HALF_CHUNK), f32),
        extra_in=pltpu.VMEM((CHUNKS, GIVEN, HALF_CHUNK), f32),
        far_out=pltpu.VMEM((2, CHUNKS, QUARTER, HALF_CHUNK), f32),
        far_in=pltpu.VMEM((CHUNKS, 2, QUARTER, HALF_CHUNK), f32),
        kept=pltpu.VMEM((CHUNKS, QUARTER, CHUNK), f32),
        load_sem=copies((10,)),
        out_load_sem=copies((CHUNKS,)),
        route_send=copies((len(PIECES),)),
        route_recv=copies((len(PIECES),)),
        near_send=copies((len(PIECES), 2)),
        near_recv=copies((len(PIECES), 2)),
        far_send=copies((len(PIECES), 2)),
        far_recv=copies((len(PIECES), 2)),
        pass_send=copies((len(PIECES), 2)),
        pass_recv=copies((len(PIECES), 2)),
        gather_send=copies((gather_sends,)),
        gather_recv=copies((SEQ, 2)),
        given_sem=copies((2,)),
        near_sum_send=copies((CHUNKS,)),
        near_sum_recv=copies((CHUNKS,)),
        extra_send=copies((CHUNKS,)),
        extra_recv=copies((CHUNKS,)),
        far_sum_send=copies((2, CHUNKS, 2)),
        far_sum_recv=copies((CHUNKS, 2, 2)),
    )


class Refs:
    def __init__(self, **refs):
        self.__dict__.update(refs)


def places():
    me = lax.axis_index("seq")
    head = lax.axis_index("head")
    sibling = head + 1 - 2 * (head % 2)
    return me, head, sibling, (head + 2) % 4, (sibling + 2) % 4


def frame_of(device, place):
    if place < HALF:
        return device * HALF + place
    return (2 * SEQ - 1 - device) * HALF + place - HALF


def angles(r):
    me = lax.axis_index("seq")
    inverse = r.inverse[...]
    for block in range(2):
        first = (me if block == 0 else 2 * SEQ - 1 - me) * BLOCK
        position = first + lax.broadcasted_iota(jnp.int32, (BLOCK, HD), 0)
        angle = position.astype(jnp.float32) * inverse
        rows = pl.ds(block * BLOCK, BLOCK)
        r.cosine[rows, :] = jnp.cos(angle)
        lane = lax.broadcasted_iota(jnp.int32, (BLOCK, HD), 1)
        turned = jnp.sin(angle)
        r.sine[rows, :] = jnp.where(lane < HD // 2, -turned, turned)


def row_of(ref, first, width):
    return ref[pl.ds(first, width)].astype(jnp.float32).reshape(1, width)


def features(r, key_loads, send_block):
    me, head, sibling, pair, cross = places()
    send = [getattr(r, f"send{k}") for k in range(len(PIECES))]
    recv = [getattr(r, f"recv{k}") for k in range(len(PIECES))]
    feat = [getattr(r, f"feat{k}") for k in range(len(PIECES))]

    def pick(device, carry):
        slot = jnp.int32(0)
        for place in range(FR_DEV):
            value = r.source_ref[frame_of(device, place)]
            slot += jnp.where(
                lax.shift_right_logical(value, 4) == me, jnp.bitwise_and(value, 15), 0
            )
        for k, (first, width) in enumerate(PIECES):
            send[k][device] = r.visual[slot, :, pl.ds(first, width)]
        return carry

    lax.fori_loop(0, SEQ, pick, 0)
    pl.semaphore_wait(pltpu.get_barrier_semaphore(), SEQ + 4)

    def route(k, j):
        device = (me + j) % SEQ
        return remote(
            send[k].at[device],
            recv[k].at[me],
            r.route_send.at[k],
            r.route_recv.at[k],
            device,
            route_head(device),
        )

    def routed(k):
        return remote(
            send[k].at[pl.ds(0, SEQ - 1)],
            recv[k].at[pl.ds(0, SEQ - 1)],
            r.route_send.at[k],
            r.route_recv.at[k],
            me,
            sibling,
        )

    for k in range(len(PIECES)):

        def start_route(j, carry):
            route(k, j).start()
            return carry

        lax.fori_loop(1, SEQ, start_route, 0)
        recv[k][me] = send[k][me]
    angles(r)

    def part_copy(label, k, half, sends, recvs, to):
        block = feat[k].at[label, pl.ds(half * BLOCK, BLOCK), :]
        return remote(block, block, sends.at[k, half], recvs.at[k, half], me, to)

    def far(label, k, half):
        return part_copy(label, k, half, r.far_send, r.far_recv, pair)

    def near_part(label, k, half):
        return part_copy(label, k, half, r.near_send, r.near_recv, sibling)

    def passed(label, k, half):
        return part_copy(label, k, half, r.pass_send, r.pass_recv, sibling)

    def add_squares(k, label, half):
        rows = pl.ds(half * BLOCK, BLOCK)
        value = feat[k][label, rows, :].astype(jnp.float32)
        value = value * value
        total = value[:, :HD]
        for first in range(HD, PIECES[k][1], HD):
            total = total + value[:, first : first + HD]
        r.squares[rows, :] += total

    r.squares[...] = jnp.zeros_like(r.squares)
    for k in range(len(PIECES)):
        routed(k).wait_recv()
        for half in range(2):
            for place in range(half * HALF, half * HALF + HALF):
                source = lax.shift_right_logical(r.source_ref[frame_of(me, place)], 4)
                feat[k][head, pl.ds(place * FT, FT), :] = recv[k][source]
            far(head, k, half).start()
            near_part(head, k, half).start()
        for half in range(2):
            add_squares(k, head, half)

    def arrive(k, half):
        far(pair, k, half).wait_recv()
        passed(pair, k, half).start()
        add_squares(k, pair, half)
        near_part(sibling, k, half).wait_recv()
        add_squares(k, sibling, half)

    def arrive_passed(k, half):
        passed(cross, k, half).wait_recv()
        add_squares(k, cross, half)

    def normalize(place, carry):
        rows = pl.ds(pl.multiple_of(place * FT, FT), FT)
        frame = jnp.where(
            place < HALF, me * HALF + place, (2 * SEQ - 1 - me) * HALF + place - HALF
        )
        swapped = lax.shift_right_logical(r.source_ref[frame], 8) != me // 16
        total = jnp.sum(r.squares[rows, :], axis=1, keepdims=True)
        factor = lax.rsqrt(total * (1.0 / MODEL) + 1e-06)
        for k, (first, width) in enumerate(PIECES):
            for part in range(2):
                one = feat[k][part, rows, :]
                two = feat[k][part + 2, rows, :]
                halves = (jnp.where(swapped, two, one), jnp.where(swapped, one, two))
                for i, value in enumerate(halves):
                    column = (part + 2 * i) * PART + first
                    scaled = value.astype(jnp.float32) * factor * row_of(r.gain, column, width)
                    r.normed[rows, pl.ds(column, width)] = scaled.astype(jnp.bfloat16)
        return carry

    last = len(PIECES) - 1
    steps = [(k, half) for k in range(last) for half in range(2)]
    for k, half in steps:
        arrive(k, half)
    for half in range(2):
        for k in range(last):
            arrive_passed(k, half)
    for load in key_loads:
        load.wait()
    for half in range(2):
        arrive(last, half)
        arrive_passed(last, half)
        lax.fori_loop(half * HALF, half * HALF + HALF, normalize, 0)
        project_keys(r, half)
        for block, target in FIRST_SENDS:
            if block == half:
                send_block((0, 0, 0), block, target)

    def finish():
        for k in range(len(PIECES)):
            routed(k).wait_send()
            for half in range(2):
                far(head, k, half).wait_send()
                near_part(head, k, half).wait_send()
                passed(pair, k, half).wait_send()

    return finish


def route_head(device):
    me, head, _, pair, _ = places()
    return jnp.where(device // 16 == me // 16, head, pair)


def rope(r, value, block):
    rows = pl.ds(block * BLOCK, BLOCK)
    turned = pltpu.roll(value, HD // 2, 1) * r.sine[rows, :]
    return (value * r.cosine[rows, :] + turned).astype(jnp.bfloat16)


def project_keys(r, block):
    me = lax.axis_index("seq")
    rows = pl.ds(block * BLOCK, BLOCK)
    part = jnp.dot(r.normed[rows, :], r.w_kv[...], preferred_element_type=jnp.float32)
    r.buf[me, block, 0] = rope(r, part[:, :HD] + row_of(r.k_bias, 0, HD), block)
    r.buf[me, block, 1] = (part[:, HD:] + row_of(r.v_bias, 0, HD)).astype(jnp.bfloat16)


def project_queries(r):
    for first in range(0, HEADS, 2):
        count = min(2, HEADS - first)
        columns = pl.ds(first * HD, count * HD)
        value = jnp.dot(r.normed[...], r.w_query[:, columns], preferred_element_type=jnp.float32)
        value = value + row_of(r.q_bias, first * HD, count * HD)
        for h in range(count):
            for block in range(2):
                one = value[block * BLOCK : (block + 1) * BLOCK, h * HD : (h + 1) * HD]
                r.q[block, pl.ds((first + h) * BLOCK, BLOCK), :] = rope(r, one, block)


def gather_copies(r):
    head = lax.axis_index("head")
    started = []

    def copy_of(source, block, target, send_sem):
        index = near(*source)
        one = r.buf.at[index, block]
        return remote(one, one, send_sem, r.gather_recv.at[index, block], near(*target), head)

    def send(source, block, target):
        started.append(copy_of(source, block, target, r.gather_send.at[len(started)]))
        started[-1].start()

    def finish():
        for copy in started:
            copy.wait_send()

    return copy_of, send, finish


def gather_attend(r, copy_of, send):
    me, _, _, y = coordinates()
    own = me // 4

    def attend(kind, dz, dx):
        group = near(dz, dx, 0) // 4
        unit = functools.partial(attend_unit, r.q, r.buf, r.m, r.l, r.acc)
        if (dz, dx) != (0, 0):
            which = jnp.where(group < own, 0, 1)
            if kind == 0:
                unit(1, group, 0, None)
            else:
                unit(which, group, which, None)
            return
        row = lax.broadcasted_iota(jnp.int32, (HEADS, BLOCK, 4 * BLOCK), 1)
        row = row.reshape(HEADS * BLOCK, 4 * BLOCK) + y * BLOCK
        column = lax.broadcasted_iota(jnp.int32, (HEADS * BLOCK, 4 * BLOCK), 1)
        if kind == 0:
            unit(1, group, 0, None)
        elif kind == 1:
            later = column % BLOCK - (column // BLOCK) * BLOCK
            unit(1, group, 1, later <= row - 2 * y * BLOCK)
        else:
            unit(0, group, 0, column <= row)

    plan = gather_plan()
    for code in SCHEDULE:
        if code >= 64:
            attend((code - 64) // 8, (code % 8) // 4, code % 4)
            continue
        block, source = code // 32, ((code // 16) % 2, (code // 4) % 4, code % 4)
        copy_of(source, block, (1, 0, 0), r.gather_send.at[0]).wait_recv()
        for target in plan[(block, *source)]:
            send(source, block, target)


def output(r, out):
    me, head, sibling, pair, _ = places()
    other = near(1, 0, 0)
    core = head % 2
    theirs = 2 * ((head // 2 + 1) % 2)
    for which in range(2):
        total = jnp.sum(r.l[which], axis=1, keepdims=True)
        value = (r.acc[which] / total).astype(jnp.bfloat16)
        for h in range(HEADS):
            for half in range(2):
                first = h * BLOCK + half * QUARTER
                r.heads[2 * which + half, :, pl.ds(h * HD, HD)] = value[first : first + QUARTER]
    gift = remote(
        r.heads.at[theirs + 1, pl.ds(DIRECT, GIVEN), :],
        r.given,
        r.given_sem.at[0],
        r.given_sem.at[1],
        other,
        head,
    )
    gift.start()
    for place, quarter in enumerate((theirs, sibling, head)):
        r.rows[pl.ds(place * QUARTER, QUARTER), :] = r.heads[quarter]
    r.rows[pl.ds(3 * QUARTER, DIRECT), :] = r.heads[theirs + 1, pl.ds(0, DIRECT), :]

    def near_copy(j):
        return remote(
            r.near_out.at[j],
            r.near_in.at[j],
            r.near_sum_send.at[j],
            r.near_sum_recv.at[j],
            me,
            sibling,
        )

    def extra_copy(j):
        return remote(
            r.extra_out.at[j],
            r.extra_in.at[j],
            r.extra_send.at[j],
            r.extra_recv.at[j],
            me,
            sibling,
        )

    parts = (pl.ds(0, DIRECT), pl.ds(DIRECT, GIVEN))

    def far_copy(which, j, part):
        return remote(
            r.far_out.at[which, j, parts[part], :],
            r.far_in.at[j, core, parts[part], :],
            r.far_sum_send.at[which, j, part],
            r.far_sum_recv.at[j, core, part],
            other if which and part else me,
            theirs + which,
        )

    def split(value):
        left, right = value[:, :HALF_CHUNK], value[:, HALF_CHUNK:]
        return jnp.where(core == 0, left, right), jnp.where(core == 0, right, left)

    def relay(j):
        near_copy(j).wait_recv()
        r.far_out[0, j] += r.near_in[j, pl.ds(0, QUARTER), :]
        for part in range(2):
            far_copy(0, j, part).start()
        r.far_out[1, j, parts[0], :] += r.near_in[j, pl.ds(3 * QUARTER, DIRECT), :]
        far_copy(1, j, 0).start()
        for half in range(2):
            r.kept[j, :, pl.ds(half * HALF_CHUNK, HALF_CHUNK)] += r.near_in[
                j, pl.ds((half + 1) * QUARTER, QUARTER), :
            ]

    def relay_extra(j):
        extra_copy(j).wait_recv()
        r.far_out[1, j, parts[1], :] += r.extra_in[j]
        far_copy(1, j, 1).start()

    for j in range(CHUNKS):
        value = jnp.dot(r.rows[...], r.w_out[j], preferred_element_type=jnp.float32)
        mine, handed = split(value[:QUARTER])
        r.near_out[j, pl.ds(0, QUARTER), :] = handed
        for half in range(2):
            r.near_out[j, pl.ds((half + 1) * QUARTER, QUARTER), :] = value[
                QUARTER : 2 * QUARTER, half * HALF_CHUNK : (half + 1) * HALF_CHUNK
            ]
        r.far_out[0, j] = mine
        mine, handed = split(value[3 * QUARTER :])
        r.near_out[j, pl.ds(3 * QUARTER, DIRECT), :] = handed
        near_copy(j).start()
        r.far_out[1, j, parts[0], :] = mine
        r.kept[j] = value[2 * QUARTER : 3 * QUARTER]
        if j > 0:
            relay(j - 1)
    relay(CHUNKS - 1)
    gift.wait()
    for j in range(CHUNKS):
        value = jnp.dot(r.given[...], r.w_out[j], preferred_element_type=jnp.float32)
        mine, handed = split(value)
        r.extra_out[j] = handed
        extra_copy(j).start()
        r.far_out[1, j, parts[1], :] = mine
        if j > 0:
            relay_extra(j - 1)
    relay_extra(CHUNKS - 1)
    for j in range(CHUNKS):
        for half in range(2):
            for part in range(2):
                remote(
                    r.far_out.at[0, j, parts[part], :],
                    r.far_in.at[j, half, parts[part], :],
                    r.far_sum_send.at[0, j, part],
                    r.far_sum_recv.at[j, half, part],
                    me,
                    pair,
                ).wait_recv()
            columns = pl.ds(half * HALF_CHUNK, HALF_CHUNK)
            total = r.kept[j, :, columns] + r.far_in[j, half]
            out[:, pl.ds(j * CHUNK + half * HALF_CHUNK, HALF_CHUNK)] = total.astype(jnp.bfloat16)
    for j in range(CHUNKS):
        near_copy(j).wait_send()
        extra_copy(j).wait_send()
        for which in range(2):
            for part in range(2):
                far_copy(which, j, part).wait_send()


INPUTS = (
    "source_hbm",
    "visual_hbm",
    "gain_hbm",
    "q_bias_hbm",
    "k_bias_hbm",
    "v_bias_hbm",
    "inverse_hbm",
    "query_hbm",
    "key_hbm",
    "value_hbm",
    "out_hbm",
)


def kernel(*refs):
    names = INPUTS + ("out",) + tuple(scratch())
    r = Refs(**dict(zip(names, refs)))
    me, head, sibling, pair, cross = places()
    pairs = (
        (r.source_hbm, r.source_ref),
        (r.visual_hbm, r.visual),
        (r.inverse_hbm, r.inverse),
        (r.gain_hbm, r.gain),
        (r.q_bias_hbm, r.q_bias),
        (r.k_bias_hbm, r.k_bias),
        (r.v_bias_hbm, r.v_bias),
        (r.key_hbm, r.w_kv.at[:, pl.ds(0, HD)]),
        (r.value_hbm, r.w_kv.at[:, pl.ds(HD, HD)]),
        (r.query_hbm, r.w_query),
    )
    loads = [pltpu.make_async_copy(a, b, r.load_sem.at[i]) for i, (a, b) in enumerate(pairs)]
    for j in range(CHUNKS):
        block = r.out_hbm.at[:, pl.ds(j * CHUNK, CHUNK)]
        loads.append(pltpu.make_async_copy(block, r.w_out.at[j], r.out_load_sem.at[j]))
    for load in loads[:2]:
        load.start()
    def greet_seq(j, carry):
        device = (me + j) % SEQ
        greet(barrier, device, route_head(device))
        return carry

    barrier = pltpu.get_barrier_semaphore()
    lax.fori_loop(1, SEQ, greet_seq, 0)
    for each in (sibling, pair, cross):
        greet(barrier, me, each)
    for each in (head, cross):
        greet(barrier, near(1, 0, 0), each)
    for load in loads[2:]:
        load.start()
    r.m[...] = jnp.full_like(r.m, NEG)
    r.l[...] = jnp.zeros_like(r.l)
    r.acc[...] = jnp.zeros_like(r.acc)
    for load in loads[:7]:
        load.wait()
    copy_of, send_block, gather_end = gather_copies(r)
    endings = [features(r, loads[7:9], send_block), gather_end]
    for load in loads[9:]:
        load.wait()
    project_queries(r)
    gather_attend(r, copy_of, send_block)
    output(r, r.out)
    for ending in endings:
        ending()


def on_device(
    visual, frame_source, input_norm_gain, w_query, w_key, w_value, q_bias, k_bias, v_bias, w_out
):
    inverse = 1000000.0 ** (-(np.arange(HD // 2) * 2.0) / HD)
    inverse = jnp.asarray(np.concatenate([inverse, inverse])[None], jnp.float32)
    return pl.pallas_call(
        kernel,
        out_shape=jax.ShapeDtypeStruct((QUARTER, MODEL), jnp.bfloat16),
        in_specs=[ANY] * len(INPUTS),
        out_specs=VMEM,
        scratch_shapes=list(scratch().values()),
        compiler_params=pltpu.CompilerParams(
            collective_id=1, has_side_effects=True, vmem_limit_bytes=62 << 20
        ),
    )(
        frame_source,
        visual.reshape(FR_DEV, FT, PART),
        input_norm_gain,
        q_bias,
        k_bias,
        v_bias,
        inverse,
        w_query,
        w_key,
        w_value,
        w_out,
    )


def solution(mesh):
    placed = (
        P("seq", "head"),
        P(),
        P(),
        P(None, "head"),
        P(None, "head"),
        P(None, "head"),
        P("head"),
        P("head"),
        P("head"),
        P("head", None),
    )
    return jax.shard_map(
        on_device, mesh=mesh, in_specs=placed, out_specs=P(("seq", "head"), None), check_vma=False
    )
```

```python
import functools
import math

import jax
import jax.numpy as jnp
import numpy as np
from jax import lax
from jax.experimental import pallas as pl
from jax.experimental.pallas import tpu as pltpu
from jax.sharding import PartitionSpec as P

HD = 128
HEADS = 7
FT = 16
FR_DEV = 16
HALF = FR_DEV // 2
SEQ = 32
TOK_DEV = 256
BLOCK = 128
QUARTER = 64
MODEL = 3584
PART = MODEL // 4
MESH = pl.DeviceIdType.MESH
NEG = -1e30
EXP_SCALE = math.log2(math.e) / math.sqrt(HD)
VMEM = pl.BlockSpec(memory_space=pltpu.VMEM)
ANY = pl.BlockSpec(memory_space=pl.ANY)
CHUNK = 512
CHUNKS = MODEL // CHUNK


def remote(src, dst, send_sem, recv_sem, seq, head):
    return pltpu.make_async_remote_copy(
        src_ref=src,
        dst_ref=dst,
        send_sem=send_sem,
        recv_sem=recv_sem,
        device_id=(seq, head),
        device_id_type=MESH,
    )

HALF_CHUNK = CHUNK // 2
DIRECT = 16
GIVEN = QUARTER - DIRECT
LAG = 2
PIECES = ((0, 512), (512, 384))

SCHEDULE = (
    3, 4, 35, 16, 33, 12, 2, 5, 44, 1, 48, 80, 47, 34, 8, 64,
    19, 7, 39, 51, 37, 49, 72, 15, 40, 6, 28, 45, 13, 65, 38, 36,
    9, 73, 43, 17, 20, 18, 11, 55, 68, 41, 50, 46, 29, 76, 24, 14,
    60, 67, 31, 10, 75, 42, 66, 74, 62, 53, 27, 23, 63, 22, 54, 61,
    52, 30, 71, 79, 25, 21, 56, 69, 77, 26, 58, 57, 59, 70, 78,
)
BY_Z = ((1, 0, 1), (1, 1, 2), (1, 2, 1))
PLUS = ((0, 1), (0, 2), (1, 3))
FIRST_FAR = (1, 1)


def coordinates():
    me = lax.axis_index("seq")
    return me, me // 16, (me // 4) % 4, me % 4


def near(dz, dx, dy):
    _, z, x, y = coordinates()
    return ((z + dz) % 2) * 16 + ((x + dx) % 4) * 4 + (y + dy) % 4


def comes_from(block, source):
    dz, dx, dy = source
    first, last = (dx, dy) if block == 0 else (dy, dx)
    if last == 0:
        if dz:
            return (1, 0, 0)
        step, along_x = first if first != 2 else FIRST_FAR[block], block == 0
    elif (dz, first, last) in BY_Z:
        return (1, 0, 0)
    elif last != 2:
        step, along_x = last, block == 1
    else:
        step, along_x = 1 if (dz, first) in PLUS else 3, block == 1
    return (0, step, 0) if along_x else (0, 0, step)


def gather_plan():
    plan = {}
    for block in range(2):
        for code in range(32):
            source = (code // 16, (code // 4) % 4, code % 4)
            targets = []
            for step in ((1, 0, 0), (0, 1, 0), (0, 3, 0), (0, 0, 1), (0, 0, 3)):
                back = ((2 - step[0]) % 2, (4 - step[1]) % 4, (4 - step[2]) % 4)
                seen = (
                    (source[0] - step[0]) % 2,
                    (source[1] - step[1]) % 4,
                    (source[2] - step[2]) % 4,
                )
                if seen != (0, 0, 0) and comes_from(block, seen) == back:
                    targets.append(step)
            plan[(block, *source)] = targets
    return plan


def attend_unit(q, buf, m, l, acc, which, group, block, keep):
    keys = buf[pl.ds(group * 4, 4), block, 0].reshape(4 * BLOCK, HD)
    vals = buf[pl.ds(group * 4, 4), block, 1].reshape(4 * BLOCK, HD)
    s = lax.dot_general(
        q[which], keys, (((1,), (1,)), ((), ())), preferred_element_type=jnp.float32
    )
    if keep is not None:
        s = jnp.where(keep, s, NEG)
    old = m[which]
    new = jnp.maximum(old, jnp.max(s, axis=1, keepdims=True))
    fade = jnp.exp2((old - new) * EXP_SCALE)
    p = jnp.exp2((s - jnp.concatenate([new] * 4, axis=1)) * EXP_SCALE)
    parts = p[:, :128] + p[:, 128:256] + p[:, 256:384] + p[:, 384:]
    l[which] = l[which] * fade + parts
    acc[which] = acc[which] * fade + jnp.dot(
        p.astype(jnp.bfloat16), vals, preferred_element_type=jnp.float32
    )
    m[which] = new


FIRST_SENDS = (
    (0, (1, 0, 0)),
    (1, (0, 0, 1)),
    (1, (0, 3, 0)),
    (1, (0, 1, 0)),
    (0, (0, 3, 0)),
    (0, (0, 0, 3)),
    (1, (0, 0, 3)),
    (0, (0, 1, 0)),
    (0, (0, 0, 1)),
    (1, (1, 0, 0)),
)


def greet(barrier, seq, head):
    pl.semaphore_signal(barrier, inc=1, device_id=(seq, head), device_id_type=MESH)


def scratch():
    copies = pltpu.SemaphoreType.DMA
    bf16 = jnp.bfloat16
    f32 = jnp.float32
    gather_sends = sum(len(targets) for targets in gather_plan().values())
    state = pltpu.VMEM((2, HEADS * BLOCK, HD), f32)
    return dict(
        source_ref=pltpu.SMEM((SEQ * FR_DEV,), jnp.int32),
        visual=pltpu.VMEM((FR_DEV, FT, PART), bf16),
        gain=pltpu.VMEM((MODEL,), bf16),
        q_bias=pltpu.VMEM((PART,), bf16),
        k_bias=pltpu.VMEM((HD,), bf16),
        v_bias=pltpu.VMEM((HD,), bf16),
        inverse=pltpu.VMEM((1, HD), f32),
        **{f"send{k}": pltpu.VMEM((SEQ, FT, w), bf16) for k, (_, w) in enumerate(PIECES)},
        **{f"recv{k}": pltpu.VMEM((SEQ, FT, w), bf16) for k, (_, w) in enumerate(PIECES)},
        **{f"feat{k}": pltpu.VMEM((4, TOK_DEV, w), bf16) for k, (_, w) in enumerate(PIECES)},
        squares=pltpu.VMEM((TOK_DEV, HD), f32),
        normed=pltpu.VMEM((TOK_DEV, MODEL), bf16),
        w_query=pltpu.VMEM((MODEL, PART), bf16),
        w_kv=pltpu.VMEM((MODEL, 2 * HD), bf16),
        w_out=pltpu.VMEM((CHUNKS, PART, CHUNK), bf16),
        cosine=pltpu.VMEM((TOK_DEV, HD), f32),
        sine=pltpu.VMEM((TOK_DEV, HD), f32),
        q=pltpu.VMEM((2, HEADS * BLOCK, HD), bf16),
        buf=pltpu.VMEM((SEQ, 2, 2, BLOCK, HD), bf16),
        m=state,
        l=state,
        acc=state,
        heads=pltpu.VMEM((4, QUARTER, PART), bf16),
        rows=pltpu.VMEM((3 * QUARTER + DIRECT, PART), bf16),
        given=pltpu.VMEM((GIVEN, PART), bf16),
        near_out=pltpu.VMEM((CHUNKS, 3 * QUARTER + DIRECT, HALF_CHUNK), f32),
        near_in=pltpu.VMEM((CHUNKS, 3 * QUARTER + DIRECT, HALF_CHUNK), f32),
        extra_out=pltpu.VMEM((CHUNKS, GIVEN, HALF_CHUNK), f32),
        extra_in=pltpu.VMEM((CHUNKS, GIVEN, HALF_CHUNK), f32),
        far_out=pltpu.VMEM((2, CHUNKS, QUARTER, HALF_CHUNK), f32),
        far_in=pltpu.VMEM((CHUNKS, 2, QUARTER, HALF_CHUNK), f32),
        kept=pltpu.VMEM((CHUNKS, QUARTER, CHUNK), f32),
        load_sem=copies((10,)),
        out_load_sem=copies((CHUNKS,)),
        route_send=copies((len(PIECES),)),
        route_recv=copies((len(PIECES),)),
        near_send=copies((len(PIECES), 2)),
        near_recv=copies((len(PIECES), 2)),
        far_send=copies((len(PIECES), 2)),
        far_recv=copies((len(PIECES), 2)),
        pass_send=copies((len(PIECES), 2)),
        pass_recv=copies((len(PIECES), 2)),
        gather_send=copies((gather_sends,)),
        gather_recv=copies((SEQ, 2)),
        given_sem=copies((2,)),
        near_sum_send=copies((CHUNKS,)),
        near_sum_recv=copies((CHUNKS,)),
        extra_send=copies((CHUNKS,)),
        extra_recv=copies((CHUNKS,)),
        far_sum_send=copies((2, CHUNKS, 2)),
        far_sum_recv=copies((CHUNKS, 2, 2)),
    )


class Refs:
    def __init__(self, **refs):
        self.__dict__.update(refs)


def places():
    me = lax.axis_index("seq")
    head = lax.axis_index("head")
    sibling = head + 1 - 2 * (head % 2)
    return me, head, sibling, (head + 2) % 4, (sibling + 2) % 4


def frame_of(device, place):
    if place < HALF:
        return device * HALF + place
    return (2 * SEQ - 1 - device) * HALF + place - HALF


def angles(r):
    me = lax.axis_index("seq")
    inverse = r.inverse[...]
    for block in range(2):
        first = (me if block == 0 else 2 * SEQ - 1 - me) * BLOCK
        position = first + lax.broadcasted_iota(jnp.int32, (BLOCK, HD), 0)
        angle = position.astype(jnp.float32) * inverse
        rows = pl.ds(block * BLOCK, BLOCK)
        r.cosine[rows, :] = jnp.cos(angle)
        lane = lax.broadcasted_iota(jnp.int32, (BLOCK, HD), 1)
        turned = jnp.sin(angle)
        r.sine[rows, :] = jnp.where(lane < HD // 2, -turned, turned)


def row_of(ref, first, width):
    return ref[pl.ds(first, width)].astype(jnp.float32).reshape(1, width)


def features(r, key_loads, send_block):
    me, head, sibling, pair, cross = places()
    send = [getattr(r, f"send{k}") for k in range(len(PIECES))]
    recv = [getattr(r, f"recv{k}") for k in range(len(PIECES))]
    feat = [getattr(r, f"feat{k}") for k in range(len(PIECES))]

    def pick(device, carry):
        slot = jnp.int32(0)
        for place in range(FR_DEV):
            value = r.source_ref[frame_of(device, place)]
            slot += jnp.where(
                lax.shift_right_logical(value, 4) == me, jnp.bitwise_and(value, 15), 0
            )
        for k, (first, width) in enumerate(PIECES):
            send[k][device] = r.visual[slot, :, pl.ds(first, width)]
        return carry

    lax.fori_loop(0, SEQ, pick, 0)
    pl.semaphore_wait(pltpu.get_barrier_semaphore(), SEQ + 4)

    def route(k, j):
        device = (me + j) % SEQ
        return remote(
            send[k].at[device],
            recv[k].at[me],
            r.route_send.at[k],
            r.route_recv.at[k],
            device,
            route_head(device),
        )

    def routed(k):
        return remote(
            send[k].at[pl.ds(0, SEQ - 1)],
            recv[k].at[pl.ds(0, SEQ - 1)],
            r.route_send.at[k],
            r.route_recv.at[k],
            me,
            sibling,
        )

    for k in range(len(PIECES)):

        def start_route(j, carry):
            route(k, j).start()
            return carry

        lax.fori_loop(1, SEQ, start_route, 0)
        recv[k][me] = send[k][me]
    angles(r)

    def part_copy(label, k, half, sends, recvs, to):
        block = feat[k].at[label, pl.ds(half * BLOCK, BLOCK), :]
        return remote(block, block, sends.at[k, half], recvs.at[k, half], me, to)

    def far(label, k, half):
        return part_copy(label, k, half, r.far_send, r.far_recv, pair)

    def near_part(label, k, half):
        return part_copy(label, k, half, r.near_send, r.near_recv, sibling)

    def passed(label, k, half):
        return part_copy(label, k, half, r.pass_send, r.pass_recv, sibling)

    def add_squares(k, label, half):
        rows = pl.ds(half * BLOCK, BLOCK)
        value = feat[k][label, rows, :].astype(jnp.float32)
        value = value * value
        total = value[:, :HD]
        for first in range(HD, PIECES[k][1], HD):
            total = total + value[:, first : first + HD]
        r.squares[rows, :] += total

    r.squares[...] = jnp.zeros_like(r.squares)
    for k in range(len(PIECES)):
        routed(k).wait_recv()
        for half in range(2):
            for place in range(half * HALF, half * HALF + HALF):
                source = lax.shift_right_logical(r.source_ref[frame_of(me, place)], 4)
                feat[k][head, pl.ds(place * FT, FT), :] = recv[k][source]
            far(head, k, half).start()
            near_part(head, k, half).start()
        for half in range(2):
            add_squares(k, head, half)

    def arrive(k, half):
        far(pair, k, half).wait_recv()
        passed(pair, k, half).start()
        add_squares(k, pair, half)
        near_part(sibling, k, half).wait_recv()
        add_squares(k, sibling, half)

    def arrive_passed(k, half):
        passed(cross, k, half).wait_recv()
        add_squares(k, cross, half)

    def normalize(place, carry):
        rows = pl.ds(pl.multiple_of(place * FT, FT), FT)
        frame = jnp.where(
            place < HALF, me * HALF + place, (2 * SEQ - 1 - me) * HALF + place - HALF
        )
        swapped = lax.shift_right_logical(r.source_ref[frame], 8) != me // 16
        total = jnp.sum(r.squares[rows, :], axis=1, keepdims=True)
        factor = lax.rsqrt(total * (1.0 / MODEL) + 1e-06)
        for k, (first, width) in enumerate(PIECES):
            for part in range(2):
                one = feat[k][part, rows, :]
                two = feat[k][part + 2, rows, :]
                halves = (jnp.where(swapped, two, one), jnp.where(swapped, one, two))
                for i, value in enumerate(halves):
                    column = (part + 2 * i) * PART + first
                    scaled = value.astype(jnp.float32) * factor * row_of(r.gain, column, width)
                    r.normed[rows, pl.ds(column, width)] = scaled.astype(jnp.bfloat16)
        return carry

    last = len(PIECES) - 1
    steps = [(k, half) for k in range(last) for half in range(2)]
    for k, half in steps:
        arrive(k, half)
    for half in range(2):
        for k in range(last):
            arrive_passed(k, half)
    for load in key_loads:
        load.wait()
    for half in range(2):
        arrive(last, half)
        arrive_passed(last, half)
        lax.fori_loop(half * HALF, half * HALF + HALF, normalize, 0)
        project_keys(r, half)
        for block, target in FIRST_SENDS:
            if block == half:
                send_block((0, 0, 0), block, target)

    def finish():
        for k in range(len(PIECES)):
            routed(k).wait_send()
            for half in range(2):
                far(head, k, half).wait_send()
                near_part(head, k, half).wait_send()
                passed(pair, k, half).wait_send()

    return finish


def route_head(device):
    me, head, _, pair, _ = places()
    return jnp.where(device // 16 == me // 16, head, pair)


def rope(r, value, block):
    rows = pl.ds(block * BLOCK, BLOCK)
    turned = pltpu.roll(value, HD // 2, 1) * r.sine[rows, :]
    return (value * r.cosine[rows, :] + turned).astype(jnp.bfloat16)


def project_keys(r, block):
    me = lax.axis_index("seq")
    rows = pl.ds(block * BLOCK, BLOCK)
    part = jnp.dot(r.normed[rows, :], r.w_kv[...], preferred_element_type=jnp.float32)
    r.buf[me, block, 0] = rope(r, part[:, :HD] + row_of(r.k_bias, 0, HD), block)
    r.buf[me, block, 1] = (part[:, HD:] + row_of(r.v_bias, 0, HD)).astype(jnp.bfloat16)


def project_queries(r):
    for first in range(0, HEADS, 2):
        count = min(2, HEADS - first)
        columns = pl.ds(first * HD, count * HD)
        value = jnp.dot(r.normed[...], r.w_query[:, columns], preferred_element_type=jnp.float32)
        value = value + row_of(r.q_bias, first * HD, count * HD)
        for h in range(count):
            for block in range(2):
                one = value[block * BLOCK : (block + 1) * BLOCK, h * HD : (h + 1) * HD]
                r.q[block, pl.ds((first + h) * BLOCK, BLOCK), :] = rope(r, one, block)


def gather_copies(r):
    head = lax.axis_index("head")
    started = []

    def copy_of(source, block, target, send_sem):
        index = near(*source)
        one = r.buf.at[index, block]
        return remote(one, one, send_sem, r.gather_recv.at[index, block], near(*target), head)

    def send(source, block, target):
        started.append(copy_of(source, block, target, r.gather_send.at[len(started)]))
        started[-1].start()

    def finish():
        for copy in started:
            copy.wait_send()

    return copy_of, send, finish


def gather_attend(r, copy_of, send):
    me, _, _, y = coordinates()
    own = me // 4

    def attend(kind, dz, dx):
        group = near(dz, dx, 0) // 4
        unit = functools.partial(attend_unit, r.q, r.buf, r.m, r.l, r.acc)
        if (dz, dx) != (0, 0):
            which = jnp.where(group < own, 0, 1)
            if kind == 0:
                unit(1, group, 0, None)
            else:
                unit(which, group, which, None)
            return
        row = lax.broadcasted_iota(jnp.int32, (HEADS, BLOCK, 4 * BLOCK), 1)
        row = row.reshape(HEADS * BLOCK, 4 * BLOCK) + y * BLOCK
        column = lax.broadcasted_iota(jnp.int32, (HEADS * BLOCK, 4 * BLOCK), 1)
        if kind == 0:
            unit(1, group, 0, None)
        elif kind == 1:
            later = column % BLOCK - (column // BLOCK) * BLOCK
            unit(1, group, 1, later <= row - 2 * y * BLOCK)
        else:
            unit(0, group, 0, column <= row)

    plan = gather_plan()
    for code in SCHEDULE:
        if code >= 64:
            attend((code - 64) // 8, (code % 8) // 4, code % 4)
            continue
        block, source = code // 32, ((code // 16) % 2, (code // 4) % 4, code % 4)
        copy_of(source, block, (1, 0, 0), r.gather_send.at[0]).wait_recv()
        for target in plan[(block, *source)]:
            send(source, block, target)


def output(r, out):
    me, head, sibling, pair, _ = places()
    other = near(1, 0, 0)
    core = head % 2
    theirs = 2 * ((head // 2 + 1) % 2)

    def finish_block(which):
        total = jnp.sum(r.l[which], axis=1, keepdims=True)
        value = (r.acc[which] / total).astype(jnp.bfloat16)
        for h in range(HEADS):
            for half in range(2):
                first = h * BLOCK + half * QUARTER
                r.heads[2 * which + half, :, pl.ds(h * HD, HD)] = value[first : first + QUARTER]

    finish_block(theirs // 2)
    gift = remote(
        r.heads.at[theirs + 1, pl.ds(DIRECT, GIVEN), :],
        r.given,
        r.given_sem.at[0],
        r.given_sem.at[1],
        other,
        head,
    )
    gift.start()
    finish_block(1 - theirs // 2)
    for place, quarter in enumerate((theirs, sibling, head)):
        r.rows[pl.ds(place * QUARTER, QUARTER), :] = r.heads[quarter]
    r.rows[pl.ds(3 * QUARTER, DIRECT), :] = r.heads[theirs + 1, pl.ds(0, DIRECT), :]

    def near_copy(j):
        return remote(
            r.near_out.at[j],
            r.near_in.at[j],
            r.near_sum_send.at[j],
            r.near_sum_recv.at[j],
            me,
            sibling,
        )

    def extra_copy(j):
        return remote(
            r.extra_out.at[j],
            r.extra_in.at[j],
            r.extra_send.at[j],
            r.extra_recv.at[j],
            me,
            sibling,
        )

    parts = (pl.ds(0, DIRECT), pl.ds(DIRECT, GIVEN))

    def far_copy(which, j, part):
        return remote(
            r.far_out.at[which, j, parts[part], :],
            r.far_in.at[j, core, parts[part], :],
            r.far_sum_send.at[which, j, part],
            r.far_sum_recv.at[j, core, part],
            other if which and part else me,
            theirs + which,
        )

    def split(value):
        left, right = value[:, :HALF_CHUNK], value[:, HALF_CHUNK:]
        return jnp.where(core == 0, left, right), jnp.where(core == 0, right, left)

    def relay(j):
        near_copy(j).wait_recv()
        r.far_out[0, j] += r.near_in[j, pl.ds(0, QUARTER), :]
        for part in range(2):
            far_copy(0, j, part).start()
        r.far_out[1, j, parts[0], :] += r.near_in[j, pl.ds(3 * QUARTER, DIRECT), :]
        far_copy(1, j, 0).start()
        for half in range(2):
            r.kept[j, :, pl.ds(half * HALF_CHUNK, HALF_CHUNK)] += r.near_in[
                j, pl.ds((half + 1) * QUARTER, QUARTER), :
            ]

    def relay_extra(j):
        extra_copy(j).wait_recv()
        r.far_out[1, j, parts[1], :] += r.extra_in[j]
        far_copy(1, j, 1).start()

    for j in range(CHUNKS):
        value = jnp.dot(r.rows[...], r.w_out[j], preferred_element_type=jnp.float32)
        mine, handed = split(value[:QUARTER])
        r.near_out[j, pl.ds(0, QUARTER), :] = handed
        for half in range(2):
            r.near_out[j, pl.ds((half + 1) * QUARTER, QUARTER), :] = value[
                QUARTER : 2 * QUARTER, half * HALF_CHUNK : (half + 1) * HALF_CHUNK
            ]
        r.far_out[0, j] = mine
        mine, handed = split(value[3 * QUARTER :])
        r.near_out[j, pl.ds(3 * QUARTER, DIRECT), :] = handed
        near_copy(j).start()
        r.far_out[1, j, parts[0], :] = mine
        r.kept[j] = value[2 * QUARTER : 3 * QUARTER]
        if j >= LAG:
            relay(j - LAG)
    gift.wait()
    for j in range(CHUNKS):
        value = jnp.dot(r.given[...], r.w_out[j], preferred_element_type=jnp.float32)
        mine, handed = split(value)
        r.extra_out[j] = handed
        extra_copy(j).start()
        r.far_out[1, j, parts[1], :] = mine
        if j < LAG:
            relay(CHUNKS - LAG + j)
        else:
            relay_extra(j - LAG)
    for j in range(CHUNKS - LAG, CHUNKS):
        relay_extra(j)
    for j in range(CHUNKS):
        for half in range(2):
            for part in range(2):
                remote(
                    r.far_out.at[0, j, parts[part], :],
                    r.far_in.at[j, half, parts[part], :],
                    r.far_sum_send.at[0, j, part],
                    r.far_sum_recv.at[j, half, part],
                    me,
                    pair,
                ).wait_recv()
            columns = pl.ds(half * HALF_CHUNK, HALF_CHUNK)
            total = r.kept[j, :, columns] + r.far_in[j, half]
            out[:, pl.ds(j * CHUNK + half * HALF_CHUNK, HALF_CHUNK)] = total.astype(jnp.bfloat16)
    for j in range(CHUNKS):
        near_copy(j).wait_send()
        extra_copy(j).wait_send()
        for which in range(2):
            for part in range(2):
                far_copy(which, j, part).wait_send()


INPUTS = (
    "source_hbm",
    "visual_hbm",
    "gain_hbm",
    "q_bias_hbm",
    "k_bias_hbm",
    "v_bias_hbm",
    "inverse_hbm",
    "query_hbm",
    "key_hbm",
    "value_hbm",
    "out_hbm",
)


def kernel(*refs):
    names = INPUTS + ("out",) + tuple(scratch())
    r = Refs(**dict(zip(names, refs)))
    me, head, sibling, pair, cross = places()
    pairs = (
        (r.source_hbm, r.source_ref),
        (r.visual_hbm, r.visual),
        (r.inverse_hbm, r.inverse),
        (r.gain_hbm, r.gain),
        (r.q_bias_hbm, r.q_bias),
        (r.k_bias_hbm, r.k_bias),
        (r.v_bias_hbm, r.v_bias),
        (r.key_hbm, r.w_kv.at[:, pl.ds(0, HD)]),
        (r.value_hbm, r.w_kv.at[:, pl.ds(HD, HD)]),
        (r.query_hbm, r.w_query),
    )
    loads = [pltpu.make_async_copy(a, b, r.load_sem.at[i]) for i, (a, b) in enumerate(pairs)]
    for j in range(CHUNKS):
        block = r.out_hbm.at[:, pl.ds(j * CHUNK, CHUNK)]
        loads.append(pltpu.make_async_copy(block, r.w_out.at[j], r.out_load_sem.at[j]))
    for load in loads[:2]:
        load.start()
    def greet_seq(j, carry):
        device = (me + j) % SEQ
        greet(barrier, device, route_head(device))
        return carry

    barrier = pltpu.get_barrier_semaphore()
    lax.fori_loop(1, SEQ, greet_seq, 0)
    for each in (sibling, pair, cross):
        greet(barrier, me, each)
    for each in (head, cross):
        greet(barrier, near(1, 0, 0), each)
    for load in loads[2:]:
        load.start()
    r.m[...] = jnp.full_like(r.m, NEG)
    r.l[...] = jnp.zeros_like(r.l)
    r.acc[...] = jnp.zeros_like(r.acc)
    for load in loads[:7]:
        load.wait()
    copy_of, send_block, gather_end = gather_copies(r)
    endings = [features(r, loads[7:9], send_block), gather_end]
    for load in loads[9:]:
        load.wait()
    project_queries(r)
    gather_attend(r, copy_of, send_block)
    output(r, r.out)
    for ending in endings:
        ending()


def on_device(
    visual, frame_source, input_norm_gain, w_query, w_key, w_value, q_bias, k_bias, v_bias, w_out
):
    inverse = 1000000.0 ** (-(np.arange(HD // 2) * 2.0) / HD)
    inverse = jnp.asarray(np.concatenate([inverse, inverse])[None], jnp.float32)
    return pl.pallas_call(
        kernel,
        out_shape=jax.ShapeDtypeStruct((QUARTER, MODEL), jnp.bfloat16),
        in_specs=[ANY] * len(INPUTS),
        out_specs=VMEM,
        scratch_shapes=list(scratch().values()),
        compiler_params=pltpu.CompilerParams(
            collective_id=1, has_side_effects=True, vmem_limit_bytes=62 << 20
        ),
    )(
        frame_source,
        visual.reshape(FR_DEV, FT, PART),
        input_norm_gain,
        q_bias,
        k_bias,
        v_bias,
        inverse,
        w_query,
        w_key,
        w_value,
        w_out,
    )


def solution(mesh):
    placed = (
        P("seq", "head"),
        P(),
        P(),
        P(None, "head"),
        P(None, "head"),
        P(None, "head"),
        P("head"),
        P("head"),
        P("head"),
        P("head", None),
    )
    return jax.shard_map(
        on_device, mesh=mesh, in_specs=placed, out_specs=P(("seq", "head"), None), check_vma=False
    )
```

```python
import functools
import math

import jax
import jax.numpy as jnp
import numpy as np
from jax import lax
from jax.experimental import pallas as pl
from jax.experimental.pallas import tpu as pltpu
from jax.sharding import PartitionSpec as P

HD = 128
HEADS = 7
FT = 16
FR_DEV = 16
HALF = FR_DEV // 2
SEQ = 32
TOK_DEV = 256
BLOCK = 128
QUARTER = 64
MODEL = 3584
PART = MODEL // 4
MESH = pl.DeviceIdType.MESH
NEG = -1e30
EXP_SCALE = math.log2(math.e) / math.sqrt(HD)
VMEM = pl.BlockSpec(memory_space=pltpu.VMEM)
ANY = pl.BlockSpec(memory_space=pl.ANY)
CHUNK = 512
CHUNKS = MODEL // CHUNK


def remote(src, dst, send_sem, recv_sem, seq, head):
    return pltpu.make_async_remote_copy(
        src_ref=src,
        dst_ref=dst,
        send_sem=send_sem,
        recv_sem=recv_sem,
        device_id=(seq, head),
        device_id_type=MESH,
    )

HALF_CHUNK = CHUNK // 2
DIRECT = 0
GIVEN = QUARTER - DIRECT
LAG = 2
PIECES = ((0, 512), (512, 384))

SCHEDULE = (
    3, 4, 35, 16, 33, 12, 2, 5, 44, 1, 48, 80, 47, 34, 8, 64,
    19, 7, 39, 51, 37, 49, 72, 15, 40, 6, 28, 45, 13, 65, 38, 36,
    9, 73, 43, 17, 20, 18, 11, 55, 68, 41, 50, 46, 29, 76, 24, 14,
    60, 67, 31, 10, 75, 42, 66, 74, 62, 53, 27, 23, 63, 22, 54, 61,
    52, 30, 71, 79, 25, 21, 56, 69, 77, 26, 58, 57, 59, 70, 78,
)
BY_Z = ((1, 0, 1), (1, 1, 2), (1, 2, 1))
PLUS = ((0, 1), (0, 2), (1, 3))
FIRST_FAR = (1, 1)


def coordinates():
    me = lax.axis_index("seq")
    return me, me // 16, (me // 4) % 4, me % 4


def near(dz, dx, dy):
    _, z, x, y = coordinates()
    return ((z + dz) % 2) * 16 + ((x + dx) % 4) * 4 + (y + dy) % 4


def comes_from(block, source):
    dz, dx, dy = source
    first, last = (dx, dy) if block == 0 else (dy, dx)
    if last == 0:
        if dz:
            return (1, 0, 0)
        step, along_x = first if first != 2 else FIRST_FAR[block], block == 0
    elif (dz, first, last) in BY_Z:
        return (1, 0, 0)
    elif last != 2:
        step, along_x = last, block == 1
    else:
        step, along_x = 1 if (dz, first) in PLUS else 3, block == 1
    return (0, step, 0) if along_x else (0, 0, step)


def gather_plan():
    plan = {}
    for block in range(2):
        for code in range(32):
            source = (code // 16, (code // 4) % 4, code % 4)
            targets = []
            for step in ((1, 0, 0), (0, 1, 0), (0, 3, 0), (0, 0, 1), (0, 0, 3)):
                back = ((2 - step[0]) % 2, (4 - step[1]) % 4, (4 - step[2]) % 4)
                seen = (
                    (source[0] - step[0]) % 2,
                    (source[1] - step[1]) % 4,
                    (source[2] - step[2]) % 4,
                )
                if seen != (0, 0, 0) and comes_from(block, seen) == back:
                    targets.append(step)
            plan[(block, *source)] = targets
    return plan


def attend_unit(q, buf, m, l, acc, which, group, block, keep):
    keys = buf[pl.ds(group * 4, 4), block, 0].reshape(4 * BLOCK, HD)
    vals = buf[pl.ds(group * 4, 4), block, 1].reshape(4 * BLOCK, HD)
    s = lax.dot_general(
        q[which], keys, (((1,), (1,)), ((), ())), preferred_element_type=jnp.float32
    )
    if keep is not None:
        s = jnp.where(keep, s, NEG)
    old = m[which]
    new = jnp.maximum(old, jnp.max(s, axis=1, keepdims=True))
    fade = jnp.exp2((old - new) * EXP_SCALE)
    p = jnp.exp2((s - jnp.concatenate([new] * 4, axis=1)) * EXP_SCALE)
    parts = p[:, :128] + p[:, 128:256] + p[:, 256:384] + p[:, 384:]
    l[which] = l[which] * fade + parts
    acc[which] = acc[which] * fade + jnp.dot(
        p.astype(jnp.bfloat16), vals, preferred_element_type=jnp.float32
    )
    m[which] = new


FIRST_SENDS = (
    (0, (1, 0, 0)),
    (1, (0, 0, 1)),
    (1, (0, 3, 0)),
    (1, (0, 1, 0)),
    (0, (0, 3, 0)),
    (0, (0, 0, 3)),
    (1, (0, 0, 3)),
    (0, (0, 1, 0)),
    (0, (0, 0, 1)),
    (1, (1, 0, 0)),
)


def greet(barrier, seq, head):
    pl.semaphore_signal(barrier, inc=1, device_id=(seq, head), device_id_type=MESH)


def scratch():
    copies = pltpu.SemaphoreType.DMA
    bf16 = jnp.bfloat16
    f32 = jnp.float32
    gather_sends = sum(len(targets) for targets in gather_plan().values())
    state = pltpu.VMEM((2, HEADS * BLOCK, HD), f32)
    return dict(
        source_ref=pltpu.SMEM((SEQ * FR_DEV,), jnp.int32),
        visual=pltpu.VMEM((FR_DEV, FT, PART), bf16),
        gain=pltpu.VMEM((MODEL,), bf16),
        q_bias=pltpu.VMEM((PART,), bf16),
        k_bias=pltpu.VMEM((HD,), bf16),
        v_bias=pltpu.VMEM((HD,), bf16),
        inverse=pltpu.VMEM((1, HD), f32),
        **{f"send{k}": pltpu.VMEM((SEQ, FT, w), bf16) for k, (_, w) in enumerate(PIECES)},
        **{f"recv{k}": pltpu.VMEM((SEQ, FT, w), bf16) for k, (_, w) in enumerate(PIECES)},
        **{f"feat{k}": pltpu.VMEM((4, TOK_DEV, w), bf16) for k, (_, w) in enumerate(PIECES)},
        squares=pltpu.VMEM((TOK_DEV, HD), f32),
        normed=pltpu.VMEM((TOK_DEV, MODEL), bf16),
        w_query=pltpu.VMEM((MODEL, PART), bf16),
        w_kv=pltpu.VMEM((MODEL, 2 * HD), bf16),
        w_out=pltpu.VMEM((CHUNKS, PART, CHUNK), bf16),
        cosine=pltpu.VMEM((TOK_DEV, HD), f32),
        sine=pltpu.VMEM((TOK_DEV, HD), f32),
        q=pltpu.VMEM((2, HEADS * BLOCK, HD), bf16),
        buf=pltpu.VMEM((SEQ, 2, 2, BLOCK, HD), bf16),
        m=state,
        l=state,
        acc=state,
        heads=pltpu.VMEM((4, QUARTER, PART), bf16),
        rows=pltpu.VMEM((3 * QUARTER + DIRECT, PART), bf16),
        given=pltpu.VMEM((GIVEN, PART), bf16),
        near_out=pltpu.VMEM((CHUNKS, 3 * QUARTER + DIRECT, HALF_CHUNK), f32),
        near_in=pltpu.VMEM((CHUNKS, 3 * QUARTER + DIRECT, HALF_CHUNK), f32),
        extra_out=pltpu.VMEM((CHUNKS, GIVEN, HALF_CHUNK), f32),
        extra_in=pltpu.VMEM((CHUNKS, GIVEN, HALF_CHUNK), f32),
        far_out=pltpu.VMEM((2, CHUNKS, QUARTER, HALF_CHUNK), f32),
        far_in=pltpu.VMEM((CHUNKS, 2, QUARTER, HALF_CHUNK), f32),
        kept=pltpu.VMEM((CHUNKS, QUARTER, CHUNK), f32),
        load_sem=copies((10,)),
        out_load_sem=copies((CHUNKS,)),
        route_send=copies((len(PIECES),)),
        route_recv=copies((len(PIECES),)),
        near_send=copies((len(PIECES), 2)),
        near_recv=copies((len(PIECES), 2)),
        far_send=copies((len(PIECES), 2)),
        far_recv=copies((len(PIECES), 2)),
        pass_send=copies((len(PIECES), 2)),
        pass_recv=copies((len(PIECES), 2)),
        gather_send=copies((gather_sends,)),
        gather_recv=copies((SEQ, 2)),
        given_sem=copies((2,)),
        near_sum_send=copies((CHUNKS,)),
        near_sum_recv=copies((CHUNKS,)),
        extra_send=copies((CHUNKS,)),
        extra_recv=copies((CHUNKS,)),
        far_sum_send=copies((2, CHUNKS, 2)),
        far_sum_recv=copies((CHUNKS, 2, 2)),
    )


class Refs:
    def __init__(self, **refs):
        self.__dict__.update(refs)


def places():
    me = lax.axis_index("seq")
    head = lax.axis_index("head")
    sibling = head + 1 - 2 * (head % 2)
    return me, head, sibling, (head + 2) % 4, (sibling + 2) % 4


def frame_of(device, place):
    if place < HALF:
        return device * HALF + place
    return (2 * SEQ - 1 - device) * HALF + place - HALF


def angles(r):
    me = lax.axis_index("seq")
    inverse = r.inverse[...]
    for block in range(2):
        first = (me if block == 0 else 2 * SEQ - 1 - me) * BLOCK
        position = first + lax.broadcasted_iota(jnp.int32, (BLOCK, HD), 0)
        angle = position.astype(jnp.float32) * inverse
        rows = pl.ds(block * BLOCK, BLOCK)
        r.cosine[rows, :] = jnp.cos(angle)
        lane = lax.broadcasted_iota(jnp.int32, (BLOCK, HD), 1)
        turned = jnp.sin(angle)
        r.sine[rows, :] = jnp.where(lane < HD // 2, -turned, turned)


def row_of(ref, first, width):
    return ref[pl.ds(first, width)].astype(jnp.float32).reshape(1, width)


def features(r, key_loads, send_block):
    me, head, sibling, pair, cross = places()
    send = [getattr(r, f"send{k}") for k in range(len(PIECES))]
    recv = [getattr(r, f"recv{k}") for k in range(len(PIECES))]
    feat = [getattr(r, f"feat{k}") for k in range(len(PIECES))]

    def pick(device, carry):
        slot = jnp.int32(0)
        for place in range(FR_DEV):
            value = r.source_ref[frame_of(device, place)]
            slot += jnp.where(
                lax.shift_right_logical(value, 4) == me, jnp.bitwise_and(value, 15), 0
            )
        for k, (first, width) in enumerate(PIECES):
            send[k][device] = r.visual[slot, :, pl.ds(first, width)]
        return carry

    lax.fori_loop(0, SEQ, pick, 0)
    pl.semaphore_wait(pltpu.get_barrier_semaphore(), SEQ + 4)

    def route(k, j):
        device = (me + j) % SEQ
        return remote(
            send[k].at[device],
            recv[k].at[me],
            r.route_send.at[k],
            r.route_recv.at[k],
            device,
            route_head(device),
        )

    def routed(k):
        return remote(
            send[k].at[pl.ds(0, SEQ - 1)],
            recv[k].at[pl.ds(0, SEQ - 1)],
            r.route_send.at[k],
            r.route_recv.at[k],
            me,
            sibling,
        )

    for k in range(len(PIECES)):

        def start_route(j, carry):
            route(k, j).start()
            return carry

        lax.fori_loop(1, SEQ, start_route, 0)
        recv[k][me] = send[k][me]
    angles(r)

    def part_copy(label, k, half, sends, recvs, to):
        block = feat[k].at[label, pl.ds(half * BLOCK, BLOCK), :]
        return remote(block, block, sends.at[k, half], recvs.at[k, half], me, to)

    def far(label, k, half):
        return part_copy(label, k, half, r.far_send, r.far_recv, pair)

    def near_part(label, k, half):
        return part_copy(label, k, half, r.near_send, r.near_recv, sibling)

    def passed(label, k, half):
        return part_copy(label, k, half, r.pass_send, r.pass_recv, sibling)

    def add_squares(k, label, half):
        rows = pl.ds(half * BLOCK, BLOCK)
        value = feat[k][label, rows, :].astype(jnp.float32)
        value = value * value
        total = value[:, :HD]
        for first in range(HD, PIECES[k][1], HD):
            total = total + value[:, first : first + HD]
        r.squares[rows, :] += total

    r.squares[...] = jnp.zeros_like(r.squares)
    for k in range(len(PIECES)):
        routed(k).wait_recv()
        for half in range(2):
            for place in range(half * HALF, half * HALF + HALF):
                source = lax.shift_right_logical(r.source_ref[frame_of(me, place)], 4)
                feat[k][head, pl.ds(place * FT, FT), :] = recv[k][source]
            far(head, k, half).start()
            near_part(head, k, half).start()
        for half in range(2):
            add_squares(k, head, half)

    def arrive(k, half):
        far(pair, k, half).wait_recv()
        passed(pair, k, half).start()
        add_squares(k, pair, half)
        near_part(sibling, k, half).wait_recv()
        add_squares(k, sibling, half)

    def arrive_passed(k, half):
        passed(cross, k, half).wait_recv()
        add_squares(k, cross, half)

    def normalize(place, carry):
        rows = pl.ds(pl.multiple_of(place * FT, FT), FT)
        frame = jnp.where(
            place < HALF, me * HALF + place, (2 * SEQ - 1 - me) * HALF + place - HALF
        )
        swapped = lax.shift_right_logical(r.source_ref[frame], 8) != me // 16
        total = jnp.sum(r.squares[rows, :], axis=1, keepdims=True)
        factor = lax.rsqrt(total * (1.0 / MODEL) + 1e-06)
        for k, (first, width) in enumerate(PIECES):
            for part in range(2):
                one = feat[k][part, rows, :]
                two = feat[k][part + 2, rows, :]
                halves = (jnp.where(swapped, two, one), jnp.where(swapped, one, two))
                for i, value in enumerate(halves):
                    column = (part + 2 * i) * PART + first
                    scaled = value.astype(jnp.float32) * factor * row_of(r.gain, column, width)
                    r.normed[rows, pl.ds(column, width)] = scaled.astype(jnp.bfloat16)
        return carry

    last = len(PIECES) - 1
    steps = [(k, half) for k in range(last) for half in range(2)]
    for k, half in steps:
        arrive(k, half)
    for half in range(2):
        for k in range(last):
            arrive_passed(k, half)
    for load in key_loads:
        load.wait()
    for half in range(2):
        arrive(last, half)
        arrive_passed(last, half)
        lax.fori_loop(half * HALF, half * HALF + HALF, normalize, 0)
        project_keys(r, half)
        for block, target in FIRST_SENDS:
            if block == half:
                send_block((0, 0, 0), block, target)

    def finish():
        for k in range(len(PIECES)):
            routed(k).wait_send()
            for half in range(2):
                far(head, k, half).wait_send()
                near_part(head, k, half).wait_send()
                passed(pair, k, half).wait_send()

    return finish


def route_head(device):
    me, head, _, pair, _ = places()
    return jnp.where(device // 16 == me // 16, head, pair)


def rope(r, value, block):
    rows = pl.ds(block * BLOCK, BLOCK)
    turned = pltpu.roll(value, HD // 2, 1) * r.sine[rows, :]
    return (value * r.cosine[rows, :] + turned).astype(jnp.bfloat16)


def project_keys(r, block):
    me = lax.axis_index("seq")
    rows = pl.ds(block * BLOCK, BLOCK)
    part = jnp.dot(r.normed[rows, :], r.w_kv[...], preferred_element_type=jnp.float32)
    r.buf[me, block, 0] = rope(r, part[:, :HD] + row_of(r.k_bias, 0, HD), block)
    r.buf[me, block, 1] = (part[:, HD:] + row_of(r.v_bias, 0, HD)).astype(jnp.bfloat16)


def project_queries(r):
    for first in range(0, HEADS, 2):
        count = min(2, HEADS - first)
        columns = pl.ds(first * HD, count * HD)
        value = jnp.dot(r.normed[...], r.w_query[:, columns], preferred_element_type=jnp.float32)
        value = value + row_of(r.q_bias, first * HD, count * HD)
        for h in range(count):
            for block in range(2):
                one = value[block * BLOCK : (block + 1) * BLOCK, h * HD : (h + 1) * HD]
                r.q[block, pl.ds((first + h) * BLOCK, BLOCK), :] = rope(r, one, block)


def gather_copies(r):
    head = lax.axis_index("head")
    started = []

    def copy_of(source, block, target, send_sem):
        index = near(*source)
        one = r.buf.at[index, block]
        return remote(one, one, send_sem, r.gather_recv.at[index, block], near(*target), head)

    def send(source, block, target):
        started.append(copy_of(source, block, target, r.gather_send.at[len(started)]))
        started[-1].start()

    def finish():
        for copy in started:
            copy.wait_send()

    return copy_of, send, finish


def gather_attend(r, copy_of, send):
    me, _, _, y = coordinates()
    own = me // 4

    def attend(kind, dz, dx):
        group = near(dz, dx, 0) // 4
        unit = functools.partial(attend_unit, r.q, r.buf, r.m, r.l, r.acc)
        if (dz, dx) != (0, 0):
            which = jnp.where(group < own, 0, 1)
            if kind == 0:
                unit(1, group, 0, None)
            else:
                unit(which, group, which, None)
            return
        row = lax.broadcasted_iota(jnp.int32, (HEADS, BLOCK, 4 * BLOCK), 1)
        row = row.reshape(HEADS * BLOCK, 4 * BLOCK) + y * BLOCK
        column = lax.broadcasted_iota(jnp.int32, (HEADS * BLOCK, 4 * BLOCK), 1)
        if kind == 0:
            unit(1, group, 0, None)
        elif kind == 1:
            later = column % BLOCK - (column // BLOCK) * BLOCK
            unit(1, group, 1, later <= row - 2 * y * BLOCK)
        else:
            unit(0, group, 0, column <= row)

    plan = gather_plan()
    for code in SCHEDULE:
        if code >= 64:
            attend((code - 64) // 8, (code % 8) // 4, code % 4)
            continue
        block, source = code // 32, ((code // 16) % 2, (code // 4) % 4, code % 4)
        copy_of(source, block, (1, 0, 0), r.gather_send.at[0]).wait_recv()
        for target in plan[(block, *source)]:
            send(source, block, target)


def output(r, out):
    me, head, sibling, pair, _ = places()
    other = near(1, 0, 0)
    core = head % 2
    theirs = 2 * ((head // 2 + 1) % 2)

    def finish_block(which):
        total = jnp.sum(r.l[which], axis=1, keepdims=True)
        value = (r.acc[which] / total).astype(jnp.bfloat16)
        for h in range(HEADS):
            for half in range(2):
                first = h * BLOCK + half * QUARTER
                r.heads[2 * which + half, :, pl.ds(h * HD, HD)] = value[first : first + QUARTER]

    finish_block(theirs // 2)
    gift = remote(
        r.heads.at[theirs + 1, pl.ds(DIRECT, GIVEN), :],
        r.given,
        r.given_sem.at[0],
        r.given_sem.at[1],
        other,
        head,
    )
    gift.start()
    finish_block(1 - theirs // 2)
    for place, quarter in enumerate((theirs, sibling, head)):
        r.rows[pl.ds(place * QUARTER, QUARTER), :] = r.heads[quarter]

    def near_copy(j):
        return remote(
            r.near_out.at[j],
            r.near_in.at[j],
            r.near_sum_send.at[j],
            r.near_sum_recv.at[j],
            me,
            sibling,
        )

    def extra_copy(j):
        return remote(
            r.extra_out.at[j],
            r.extra_in.at[j],
            r.extra_send.at[j],
            r.extra_recv.at[j],
            me,
            sibling,
        )

    parts = (pl.ds(0, QUARTER // 2), pl.ds(QUARTER // 2, QUARTER // 2))

    def far_copy(which, j, part):
        return remote(
            r.far_out.at[which, j, parts[part], :],
            r.far_in.at[j, core, parts[part], :],
            r.far_sum_send.at[which, j, part],
            r.far_sum_recv.at[j, core, part],
            other if which else me,
            theirs + which,
        )

    def split(value):
        left, right = value[:, :HALF_CHUNK], value[:, HALF_CHUNK:]
        return jnp.where(core == 0, left, right), jnp.where(core == 0, right, left)

    def relay(j):
        near_copy(j).wait_recv()
        r.far_out[0, j] += r.near_in[j, pl.ds(0, QUARTER), :]
        for part in range(2):
            far_copy(0, j, part).start()
        for half in range(2):
            r.kept[j, :, pl.ds(half * HALF_CHUNK, HALF_CHUNK)] += r.near_in[
                j, pl.ds((half + 1) * QUARTER, QUARTER), :
            ]

    def relay_extra(j):
        extra_copy(j).wait_recv()
        r.far_out[1, j] += r.extra_in[j]
        for part in range(2):
            far_copy(1, j, part).start()

    for j in range(CHUNKS):
        value = jnp.dot(r.rows[...], r.w_out[j], preferred_element_type=jnp.float32)
        mine, handed = split(value[:QUARTER])
        r.near_out[j, pl.ds(0, QUARTER), :] = handed
        for half in range(2):
            r.near_out[j, pl.ds((half + 1) * QUARTER, QUARTER), :] = value[
                QUARTER : 2 * QUARTER, half * HALF_CHUNK : (half + 1) * HALF_CHUNK
            ]
        r.far_out[0, j] = mine
        near_copy(j).start()
        r.kept[j] = value[2 * QUARTER : 3 * QUARTER]
        if j >= LAG:
            relay(j - LAG)
    gift.wait()
    for j in range(CHUNKS):
        value = jnp.dot(r.given[...], r.w_out[j], preferred_element_type=jnp.float32)
        mine, handed = split(value)
        r.extra_out[j] = handed
        extra_copy(j).start()
        r.far_out[1, j] = mine
        if j < LAG:
            relay(CHUNKS - LAG + j)
        else:
            relay_extra(j - LAG)
    for j in range(CHUNKS - LAG, CHUNKS):
        relay_extra(j)
    for j in range(CHUNKS):
        for half in range(2):
            for part in range(2):
                remote(
                    r.far_out.at[0, j, parts[part], :],
                    r.far_in.at[j, half, parts[part], :],
                    r.far_sum_send.at[0, j, part],
                    r.far_sum_recv.at[j, half, part],
                    me,
                    pair,
                ).wait_recv()
            columns = pl.ds(half * HALF_CHUNK, HALF_CHUNK)
            total = r.kept[j, :, columns] + r.far_in[j, half]
            out[:, pl.ds(j * CHUNK + half * HALF_CHUNK, HALF_CHUNK)] = total.astype(jnp.bfloat16)
    for j in range(CHUNKS):
        near_copy(j).wait_send()
        extra_copy(j).wait_send()
        for which in range(2):
            for part in range(2):
                far_copy(which, j, part).wait_send()


INPUTS = (
    "source_hbm",
    "visual_hbm",
    "gain_hbm",
    "q_bias_hbm",
    "k_bias_hbm",
    "v_bias_hbm",
    "inverse_hbm",
    "query_hbm",
    "key_hbm",
    "value_hbm",
    "out_hbm",
)


def kernel(*refs):
    names = INPUTS + ("out",) + tuple(scratch())
    r = Refs(**dict(zip(names, refs)))
    me, head, sibling, pair, cross = places()
    pairs = (
        (r.source_hbm, r.source_ref),
        (r.visual_hbm, r.visual),
        (r.inverse_hbm, r.inverse),
        (r.gain_hbm, r.gain),
        (r.q_bias_hbm, r.q_bias),
        (r.k_bias_hbm, r.k_bias),
        (r.v_bias_hbm, r.v_bias),
        (r.key_hbm, r.w_kv.at[:, pl.ds(0, HD)]),
        (r.value_hbm, r.w_kv.at[:, pl.ds(HD, HD)]),
        (r.query_hbm, r.w_query),
    )
    loads = [pltpu.make_async_copy(a, b, r.load_sem.at[i]) for i, (a, b) in enumerate(pairs)]
    for j in range(CHUNKS):
        block = r.out_hbm.at[:, pl.ds(j * CHUNK, CHUNK)]
        loads.append(pltpu.make_async_copy(block, r.w_out.at[j], r.out_load_sem.at[j]))
    for load in loads[:2]:
        load.start()
    def greet_seq(j, carry):
        device = (me + j) % SEQ
        greet(barrier, device, route_head(device))
        return carry

    barrier = pltpu.get_barrier_semaphore()
    lax.fori_loop(1, SEQ, greet_seq, 0)
    for each in (sibling, pair, cross):
        greet(barrier, me, each)
    for each in (head, cross):
        greet(barrier, near(1, 0, 0), each)
    for load in loads[2:]:
        load.start()
    r.m[...] = jnp.full_like(r.m, NEG)
    r.l[...] = jnp.zeros_like(r.l)
    r.acc[...] = jnp.zeros_like(r.acc)
    for load in loads[:7]:
        load.wait()
    copy_of, send_block, gather_end = gather_copies(r)
    endings = [features(r, loads[7:9], send_block), gather_end]
    for load in loads[9:]:
        load.wait()
    project_queries(r)
    gather_attend(r, copy_of, send_block)
    output(r, r.out)
    for ending in endings:
        ending()


def on_device(
    visual, frame_source, input_norm_gain, w_query, w_key, w_value, q_bias, k_bias, v_bias, w_out
):
    inverse = 1000000.0 ** (-(np.arange(HD // 2) * 2.0) / HD)
    inverse = jnp.asarray(np.concatenate([inverse, inverse])[None], jnp.float32)
    return pl.pallas_call(
        kernel,
        out_shape=jax.ShapeDtypeStruct((QUARTER, MODEL), jnp.bfloat16),
        in_specs=[ANY] * len(INPUTS),
        out_specs=VMEM,
        scratch_shapes=list(scratch().values()),
        compiler_params=pltpu.CompilerParams(
            collective_id=1, has_side_effects=True, vmem_limit_bytes=62 << 20
        ),
    )(
        frame_source,
        visual.reshape(FR_DEV, FT, PART),
        input_norm_gain,
        q_bias,
        k_bias,
        v_bias,
        inverse,
        w_query,
        w_key,
        w_value,
        w_out,
    )


def solution(mesh):
    placed = (
        P("seq", "head"),
        P(),
        P(),
        P(None, "head"),
        P(None, "head"),
        P(None, "head"),
        P("head"),
        P("head"),
        P("head"),
        P("head", None),
    )
    return jax.shard_map(
        on_device, mesh=mesh, in_specs=placed, out_specs=P(("seq", "head"), None), check_vma=False
    )
```
